256 devices in a mesh: blk: 128 (over y, z, x_lo, core), ch: 2 (over x_hi).
Axes of the slice: x: 4 (x_hi: 2, x_lo: 2; x = x_hi * 2 + x_lo), y: 4, z: 8, core: 2. Of those that a mesh axis runs over, the one named last changes fastest.
Arguments:
- record: float32 [4096, 32768], P(('blk', 'ch')), may hold values from -80 to 80, as said below
- templates: bfloat16 [1024, 512, 256], P('blk', 'ch'), may hold values from -0.015625 to 0.015625
- offsets: int32 [1024], P('blk'), may hold values from 0 to 3584
Outputs:
- scores: float32 [1024, 2, 256], P('blk', None, 'ch')
The draws below stay inside these ranges and needn't reach their ends.
Inputs may be any that keep to these rules, and one draw needn't show every extreme that they name: `record`: finite real samples.
All inputs are finite; a program needn't handle non-finite values.
Results may differ from the reference program's by a relative error of at most 0.0029.
Values may be sent and summed in bfloat16 or wider, within the bound.
A program may use at most 128 MiB of HBM per device.

```python
import math
import jax
import jax.numpy as jnp
from jax import lax

NCH = 4096
CSPAN = 512
TLEN = 256
FRAME = 128
SLAB = 256
TD = 8
ROT = 2
NT = 32768
NTEMP = 1024
N_BLK = 128


def draw_record(key, part):
    key = jax.random.fold_in(key, 11)
    key_noise, key_scale, key_color = jax.random.split(key, 3)
    frame_count = NT // FRAME
    scales = jnp.exp(jax.random.uniform(key_scale, (NCH, frame_count, 1), jnp.float32, 0.0, 2.302585))
    coloring = jax.random.uniform(key_color, (NCH, 1), jnp.float32, -0.9, 0.9)
    noise_part = jnp.clip(jax.random.normal(key_noise, (NCH, NT), jnp.float32), -4.0, 4.0)
    earlier = jnp.pad(noise_part[:, :-1], ((0, 0), (1, 0)))
    combined = noise_part + coloring * earlier
    return (combined.reshape(NCH, frame_count, FRAME) * scales).reshape(NCH, NT)


def plant(values, rng, low, high):
    index_at = [jax.random.randint(jax.random.fold_in(rng, axis), (), 0, length) for axis, length in enumerate(values.shape)]
    longest = values.shape.index(max(values.shape))
    neighbour = index_at[:longest] + [(index_at[longest] + 1) % values.shape[longest]] + index_at[longest + 1:]
    return values.at[tuple(index_at)].set(low).at[tuple(neighbour)].set(high)


def block_scale(key, extent, cuts, smallest, top_value):
    gain = 1.0
    for axis_at, parts in cuts:
        heights = jax.random.uniform(jax.random.fold_in(jax.random.fold_in(key, 6), axis_at), (parts,), jnp.float32, smallest / len(cuts), top_value / len(cuts))
        gain = gain * jnp.repeat(jnp.exp(heights), extent[axis_at] // parts).reshape((-1,) + (1,) * (len(extent) - 1 - axis_at))
    return gain


def centred(key, dims, width, limit, shards=(), kind=jnp.bfloat16):
    entries = width * jax.random.normal(key, dims, jnp.float32)
    if shards:
        entries = entries * block_scale(key, dims, shards, -0.22, 0.18)
    return jnp.clip(entries, -limit, limit).astype(kind)


def setup_inputs(seed: int = 0) -> dict:
    splits = jax.random.split(jax.random.key(seed), 4)
    return {
        "record": draw_record(jax.random.fold_in(splits[3], 71), 0),
        "templates": centred(splits[1], (NTEMP, CSPAN, TLEN), (CSPAN * TLEN) ** -0.5, 0.015625, ((0, 128), (1, 2))),
        "offsets": plant(jax.random.randint(splits[2], (NTEMP,), 0, NCH - CSPAN + 1), jax.random.fold_in(splits[2], 1), 0, NCH - CSPAN).astype(jnp.int32),
    }


eps_power = 1e-06
eps_energy = 1e-05

def dft_tables(frame_len):
    indices = jnp.arange(frame_len, dtype=jnp.int32)
    phases = indices[:, None] * indices[None, :] % frame_len
    angles = phases.astype(jnp.float32) * (2.0 * math.pi / frame_len)
    return (jnp.cos(angles), jnp.sin(angles))

def whiten(chan_block, frame_len):
    chan_count, sample_count = chan_block.shape
    cosine, sine_table = dft_tables(frame_len)
    forward = jnp.concatenate([cosine, -sine_table], axis=1)
    frames = chan_block.reshape(chan_count, sample_count // frame_len, frame_len)
    spectrum = jnp.einsum('cmn,nf->cmf', frames, forward, precision=lax.Precision.HIGHEST)
    real_part = spectrum[:, :, :frame_len]
    imag_part = spectrum[:, :, frame_len:]
    band_power = lax.optimization_barrier(jnp.mean(real_part * real_part + imag_part * imag_part, axis=1))
    inverse_amp = 1.0 / jnp.sqrt(band_power + eps_power)
    scaled = spectrum * jnp.concatenate([inverse_amp, inverse_amp], axis=1)[:, None, :]
    restored = jnp.einsum('cmf,fn->cmn', scaled, forward.T, precision=lax.Precision.HIGHEST)
    restored = restored / jnp.sqrt(jnp.float32(frame_len))
    return restored.reshape(chan_count, sample_count).astype(jnp.bfloat16)

def diagonal_sums(product, out_len):
    item_count, lag_count, wide_count = product.shape
    flattened = product.reshape(item_count, lag_count * wide_count)
    flattened = jnp.pad(flattened, ((0, 0), (0, lag_count)))
    skewed = flattened.reshape(item_count, lag_count, wide_count + 1)
    return lax.optimization_barrier(jnp.sum(skewed[:, :, :out_len], axis=1))

def window_energy(power_sum, lag_count, out_len):
    running = jnp.cumsum(power_sum, axis=1)
    running = jnp.pad(running, ((0, 0), (1, 0)))
    return running[:, lag_count:lag_count + out_len] - running[:, :out_len]

def reference(record, templates, offsets):
    channel_groups = record.reshape(NCH // 64, 64, NT)
    whitened = lax.map(lambda chan_block: whiten(chan_block, FRAME), channel_groups).reshape(NCH, NT)
    padded = jnp.concatenate([whitened, jnp.zeros((NCH, TLEN), jnp.bfloat16)], axis=1)
    shard_ids = jnp.arange(NTEMP, dtype=jnp.int32) // TD
    grouped = templates.reshape(NTEMP // 8, 8, CSPAN, TLEN)
    group_shards = shard_ids.reshape(NTEMP // 8, 8)
    group_offsets = offsets.astype(jnp.int32).reshape(NTEMP // 8, 8)

    def one_group(member):
        shapes, shard_part, offset_part = member
        results = []
        for visit in range(ROT):
            time_start = ((shard_part - visit) % N_BLK * SLAB).astype(jnp.int32)
            windows = jax.vmap(lambda chan_first, time_first: lax.dynamic_slice(padded, (chan_first.astype(jnp.int32), time_first.astype(jnp.int32)), (CSPAN, SLAB + TLEN)))(offset_part, time_start)
            wide_windows = windows.astype(jnp.float32)
            product = jnp.einsum('kcs,kcw->ksw', shapes.astype(jnp.float32), wide_windows, precision=lax.Precision.HIGHEST)
            cross_sum = diagonal_sums(product, SLAB)
            energy = window_energy(lax.optimization_barrier(jnp.sum(wide_windows * wide_windows, axis=1)), TLEN, SLAB)
            results.append(cross_sum / jnp.sqrt(energy / (CSPAN * TLEN) + eps_energy))
        return jnp.stack(results, axis=1)
    scores = lax.map(one_group, (grouped, group_shards, group_offsets))
    return scores.reshape(NTEMP, ROT, SLAB)
```

```python
import functools

import jax
import jax.numpy as jnp
import numpy as np
from jax import lax
from jax.experimental import pallas as pl
from jax.experimental.pallas import tpu as pltpu
from jax.sharding import PartitionSpec as P

MESH = pl.DeviceIdType.MESH
F32 = jnp.float32
BF16 = jnp.bfloat16

FRAME = 128
CHUNK = 16
CSPAN = 512
TLEN = 256
SLAB = 256
TD = 8
GROUP = 4
SUBS = 8
FOLD = 64
EPS_POWER = 1e-6
EPS_ENERGY = 1e-5


def transform_tables():
    n = np.arange(FRAME)
    col = np.arange(FRAME)
    freq = np.where(col <= 64, col, col - 64)
    angle = 2.0 * np.pi * ((n[:, None] * freq[None, :]) % FRAME) / FRAME
    basis = np.where(col <= 64, np.cos(angle), np.sin(angle))
    weight = np.where((col == 0) | (col == 64), 1.0, 2.0) / np.sqrt(FRAME)

    def split(table):
        high = table.astype(jnp.bfloat16)
        low = (table - high.astype(np.float64)).astype(jnp.bfloat16)
        top = np.concatenate([high, low], axis=1)
        bottom = np.concatenate([high, np.zeros_like(high)], axis=1)
        return np.concatenate([top, bottom], axis=0)

    return split(basis), split((basis * weight).T)


def split_rows(value):
    high = value.astype(BF16)
    low = (value - high.astype(F32)).astype(BF16)
    return jnp.concatenate([high, low], axis=1)


def left(value, count):
    return pltpu.roll(value, value.shape[1] - count, 1)


def kernel(
    ng, x_ref, t_ref, off_ref, wf_ref, wi_ref, o_ref,
    ys, ws, wz, wv, tsend, trecv, thalo, lhs, band, offv, offs, cb, qb, hs, hr, rs, rr,
    a_s, a_r, t_s, t_r, f_s, f_r, th_s, th_r, fh_s, fh_r, h_s, h_r, r_s, r_r, loc,
):
    b = lax.axis_index("blk")
    h = lax.axis_index("ch")
    m = lax.div(b, GROUP)
    e = lax.rem(b, GROUP)
    d = 2 * e + h
    up = lax.rem(m + 1, ng)
    down = lax.rem(m + ng - 1, ng)
    rows = CHUNK * ng
    frames = x_ref.shape[1] // FRAME
    wide = GROUP * SLAB

    def peer(sub):
        return {"blk": GROUP * m + lax.div(sub, 2), "ch": lax.rem(sub, 2)}

    def half_block(group):
        return pl.multiple_of(lax.rem(group, 2) * CHUNK, CHUNK)

    def far(group):
        return {"blk": GROUP * group + e}

    bar = pltpu.get_barrier_semaphore()

    def greet_peer(i, carry):
        pl.semaphore_signal(bar, inc=1, device_id=peer(lax.rem(d + i, SUBS)), device_id_type=MESH)
        return carry

    def greet_far(i, carry):
        pl.semaphore_signal(bar, inc=1, device_id=far(lax.rem(m + i, ng)), device_id_type=MESH)
        return carry

    lax.fori_loop(1, SUBS, greet_peer, 0)
    lax.fori_loop(1, ng, greet_far, 0)

    r_id = lax.broadcasted_iota(jnp.int32, (256, 256), 0)
    c_id = lax.broadcasted_iota(jnp.int32, (256, 256), 1)
    slot = 128 * ((r_id >> 4) & 1) + 16 * (r_id >> 5) + (r_id & 15)
    for k in range(TD):
        perm = jnp.where(((slot - c_id - off_ref[k]) & 255) == 0, 1.0, 0.0).astype(BF16)
        placed = jnp.dot(perm, t_ref[k], preferred_element_type=F32).astype(BF16)
        for s in range(SUBS):
            tsend[s, k] = placed[32 * s : 32 * s + 32]

    row8 = lax.broadcasted_iota(jnp.int32, (TD, 128), 0)
    own_off = jnp.zeros((TD, 128), jnp.int32)
    for k in range(TD):
        own_off = jnp.where(row8 == k, off_ref[k], own_off)
    offv[1 + e] = own_off

    pl.semaphore_wait(bar, SUBS - 1 + ng - 1)

    def template_copy(i):
        sub = lax.rem(d + i, SUBS)
        return pltpu.make_async_remote_copy(
            src_ref=tsend.at[sub], dst_ref=trecv.at[d], send_sem=t_s.at[sub], recv_sem=t_r.at[d],
            device_id=peer(sub), device_id_type=MESH,
        )

    def template_arrival(i):
        sub = lax.rem(d + i, SUBS)
        return pltpu.make_async_remote_copy(
            src_ref=tsend.at[sub], dst_ref=trecv.at[sub], send_sem=t_s.at[sub], recv_sem=t_r.at[sub],
            device_id=peer(sub), device_id_type=MESH,
        )

    def offset_copy(i):
        other = lax.rem(e + i, GROUP)
        return pltpu.make_async_remote_copy(
            src_ref=offv.at[1 + e], dst_ref=offv.at[1 + e], send_sem=f_s.at[other], recv_sem=f_r.at[e],
            device_id={"blk": GROUP * m + other}, device_id_type=MESH,
        )

    def offset_arrival(i):
        other = lax.rem(e + i, GROUP)
        return pltpu.make_async_remote_copy(
            src_ref=offv.at[1 + e], dst_ref=offv.at[1 + other], send_sem=f_s.at[other], recv_sem=f_r.at[other],
            device_id={"blk": GROUP * m + other}, device_id_type=MESH,
        )

    for i in range(1, GROUP):
        offset_copy(i).start()

    def start_template(i, carry):
        template_copy(i).start()
        return carry

    lax.fori_loop(1, SUBS, start_template, 0)

    step = 16
    wf = wf_ref[...]

    def forward(i, total):
        part = x_ref[:, pl.ds(pl.multiple_of(i * (step * FRAME), FRAME), step * FRAME)]
        stacked = jnp.concatenate([part[:, f * FRAME : (f + 1) * FRAME] for f in range(step)], axis=0)
        both = jnp.dot(split_rows(stacked), wf, preferred_element_type=F32)
        spec = both[:, :FRAME] + both[:, FRAME:]
        ys[pl.ds(pl.multiple_of(i * (step * CHUNK), 8), step * CHUNK), :] = spec
        return total + jnp.sum((spec * spec).reshape(step, CHUNK, FRAME), axis=0)

    total = lax.fori_loop(0, frames // step, forward, jnp.zeros((CHUNK, FRAME), F32))
    mean = total * (1.0 / frames)
    lane = lax.broadcasted_iota(jnp.int32, (CHUNK, FRAME), 1)
    power = jnp.where((lane & 63) == 0, mean, mean + pltpu.roll(mean, 64, 1))
    amp = 1.0 / jnp.sqrt(power + EPS_POWER)
    wi = wi_ref[...]

    def sample_copy(t):
        return pltpu.make_async_remote_copy(
            src_ref=ws.at[:, pl.ds(pl.multiple_of(t * wide, FRAME), wide)],
            dst_ref=wz.at[lax.div(m, 2), pl.ds(half_block(m), CHUNK), pl.ds(SLAB, wide)],
            send_sem=a_s.at[t], recv_sem=a_r.at[m], device_id=far(t), device_id_type=MESH,
        )

    def sample_arrival(t):
        return pltpu.make_async_remote_copy(
            src_ref=ws.at[:, pl.ds(pl.multiple_of(t * wide, FRAME), wide)],
            dst_ref=wz.at[lax.div(t, 2), pl.ds(half_block(t), CHUNK), pl.ds(SLAB, wide)],
            send_sem=a_s.at[t], recv_sem=a_r.at[t], device_id=far(t), device_id_type=MESH,
        )

    def back(i, carry):
        pair = lax.rem(lax.div(m, 2) + i, ng // 2)
        spec = ys[pl.ds(pl.multiple_of(pair * (step * CHUNK), 8), step * CHUNK), :]
        scaled = (spec.reshape(step, CHUNK, FRAME) * amp[None]).reshape(step * CHUNK, FRAME)
        both = jnp.dot(split_rows(scaled), wi, preferred_element_type=F32)
        white = (both[:, :FRAME] + both[:, FRAME:]).astype(BF16)
        for f in range(step):
            at = pl.multiple_of((pair * step + f) * FRAME, FRAME)
            ws[:, pl.ds(at, FRAME)] = white[f * CHUNK : (f + 1) * CHUNK]
        for q in range(2):
            t = 2 * pair + q

            @pl.when(t != m)
            def _():
                sample_copy(t).start()

        return carry

    lax.fori_loop(0, ng // 2, back, 0)

    wz[:, :, 0:SLAB] = jnp.zeros((rows // 32, 32, SLAB), BF16)
    wz[:, :, SLAB + wide : 2 * SLAB + wide] = jnp.zeros((rows // 32, 32, SLAB), BF16)
    wz[lax.div(m, 2), pl.ds(half_block(m), CHUNK), pl.ds(SLAB, wide)] = ws[
        :, pl.ds(pl.multiple_of(m * wide, FRAME), wide)
    ]
    trecv[d] = tsend[d]

    for i in range(1, GROUP):
        offset_arrival(i).wait()

    def end_template(i, carry):
        template_arrival(i).wait()
        return carry

    lax.fori_loop(1, SUBS, end_template, 0)

    def halo(side, kind):
        group = up if side == 0 else down
        first = SUBS - 2 if side == 0 else 0
        shard = GROUP if side == 0 else 1
        if kind == "t":
            src, dst, sems = trecv.at[pl.ds(first, 2)], thalo.at[side], (th_s, th_r)
        elif kind == "f":
            src, dst, sems = offv.at[shard], offv.at[(GROUP + 1) * side], (fh_s, fh_r)
        else:
            src, dst, sems = hs.at[side], hr.at[side], (h_s, h_r)
            group = down if side == 0 else up
        return pltpu.make_async_remote_copy(
            src_ref=src, dst_ref=dst, send_sem=sems[0].at[side], recv_sem=sems[1].at[side],
            device_id=far(group), device_id_type=MESH,
        )

    for side in range(2):
        halo(side, "f").start()
        halo(side, "t").start()

    w_id = lax.broadcasted_iota(jnp.int32, band.shape, 0)
    l_id = lax.broadcasted_iota(jnp.int32, band.shape, 1)
    gap = w_id - l_id
    band[...] = jnp.where((gap >= 0) & (gap < TLEN), 1.0, 0.0).astype(BF16)

    r_id = lax.broadcasted_iota(jnp.int32, (FOLD, TLEN), 0)
    s_id = lax.broadcasted_iota(jnp.int32, (FOLD, TLEN), 1)
    pick = jnp.where((s_id & (FOLD - 1)) == ((r_id & ~7) + 7 - (r_id & 7)), 1.0, 0.0).astype(BF16)
    part = lax.broadcasted_iota(jnp.int32, (2 * FOLD * 2, TLEN), 1) >> 6
    which = lax.broadcasted_iota(jnp.int32, (2 * FOLD * 2, TLEN), 0) >> 6
    keep = jnp.where(part == which, 1.0, 0.0).astype(BF16)

    def left_operand(first, second):
        both = jnp.concatenate([first, second], axis=0)
        spread = jnp.concatenate([both] * 4, axis=0) * keep
        turned = lax.dot_general(pick, spread, (((1,), (1,)), ((), ())), preferred_element_type=F32)
        return turned.astype(BF16)

    def prepare(q, carry):
        shard = lax.div(q, TD)
        k = lax.rem(q, TD)
        lhs[TD + q] = left_operand(trecv[2 * shard, k], trecv[2 * shard + 1, k])
        return carry

    lax.fori_loop(0, GROUP * TD, prepare, 0)

    for side in range(2):
        halo(side, "f").wait()
        halo(side, "t").wait()

    def prepare_halo(q, carry):
        side = lax.div(q, TD)
        k = lax.rem(q, TD)
        lhs[side * (GROUP + 1) * TD + k] = left_operand(thalo[side, 0, k], thalo[side, 1, k])
        return carry

    lax.fori_loop(0, 2 * TD, prepare_halo, 0)
    to_scalar = pltpu.make_async_copy(offv, offs, loc.at[0])
    to_scalar.start()
    to_scalar.wait()

    def shift_rows(t):
        at = pl.ds(half_block(t), CHUNK)
        block = wz[lax.div(t, 2), at, :]
        wv[lax.div(t, 2), at, :] = jnp.concatenate([block[:, FOLD:], block[:, :FOLD]], axis=1)

    shift_rows(m)

    def arrive(i, carry):
        t = lax.rem(m + i, ng)
        sample_arrival(t).wait()
        shift_rows(t)
        return carry

    lax.fori_loop(1, ng, arrive, 0)

    def correlate(shard, k, c0, width):
        off = offs[shard, k, 0]
        start = 16 * (off >> 7) + jnp.clip((off & 127) - 16 * d, 0, 16)
        r0 = start >> 5
        r1 = r0 + 1
        r2 = jnp.minimum(r0 + 2, rows // 32 - 1)
        late = lax.broadcasted_iota(jnp.int32, (32, width), 0) < (start & 31)
        cols = pl.ds(c0, width)

        def window(ref):
            b0, b1, b2 = ref[r0, :, cols], ref[r1, :, cols], ref[r2, :, cols]
            return jnp.concatenate([jnp.where(late, b1, b0), jnp.where(late, b2, b1)], axis=0)

        w = window(wz)
        v = window(wv)
        n = width - 128
        right = jnp.concatenate([w[:, :n], v[:, :n], w[:, 128:], v[:, 128:]], axis=0)
        prod = jnp.dot(lhs[shard * TD + k], right, preferred_element_type=F32)
        prod = prod[:32] + left(prod[32:], 32)
        prod = prod[:16] + left(prod[16:], 16)
        prod = prod[:8] + left(prod[8:], 8)
        prod = pltpu.roll(prod, n - 7, 1, stride=1, stride_axis=0)
        wide_w = w.astype(F32)
        return prod[:, : n - 128], jnp.sum((wide_w * wide_w).reshape(8, 8, width), axis=0)

    def window_energy(squares, width):
        high = squares.astype(BF16)
        rest = squares - high.astype(F32)
        mid = rest.astype(BF16)
        low = (rest - mid.astype(F32)).astype(BF16)
        sums = jnp.dot(
            jnp.concatenate([high, mid, low], axis=0), band[:width, : width - SLAB], preferred_element_type=F32
        )
        return sums[:TD] + sums[TD : 2 * TD] + sums[2 * TD :]

    for side in range(2):
        shard = (GROUP + 1) * side

        def edge(k, carry):
            cross, squares = correlate(shard, k, side * wide, 2 * SLAB)
            cb[shard, k, :, :SLAB] = cross
            qb[shard, k, :, : 2 * SLAB] = squares
            return carry

        lax.fori_loop(0, TD, edge, 0)
        cross = jnp.sum(cb[shard, :, :, :SLAB], axis=1)
        energy = window_energy(jnp.sum(qb[shard, :, :, : 2 * SLAB], axis=1), 2 * SLAB)
        if side == 0:
            cross = jnp.where(m == 0, 0.0, cross)
            energy = jnp.where(m == 0, 0.0, energy)
        for half in range(2):
            hs[side, 0, half] = cross[:, half * 128 : (half + 1) * 128]
            hs[side, 1, half] = energy[:, half * 128 : (half + 1) * 128]
        halo(side, "r").start()

    def inner(q, carry):
        shard = 1 + lax.div(q, TD)
        k = lax.rem(q, TD)
        cross, squares = correlate(shard, k, pl.multiple_of((shard - 1) * SLAB, SLAB), 3 * SLAB)
        cb[shard, k] = cross
        qb[shard, k] = squares
        return carry

    lax.fori_loop(0, GROUP * TD, inner, 0)

    def result_copy(sub):
        return pltpu.make_async_remote_copy(
            src_ref=rs.at[sub], dst_ref=rr.at[d], send_sem=r_s.at[sub], recv_sem=r_r.at[d],
            device_id=peer(sub), device_id_type=MESH,
        )

    def result_arrival(sub):
        return pltpu.make_async_remote_copy(
            src_ref=rs.at[sub], dst_ref=rr.at[sub], send_sem=r_s.at[sub], recv_sem=r_r.at[sub],
            device_id=peer(sub), device_id_type=MESH,
        )

    for side in range(2):
        halo(side, "r").wait()

    for own in range(GROUP):
        cross = jnp.sum(cb[1 + own], axis=1)
        energy = window_energy(jnp.sum(qb[1 + own], axis=1), 3 * SLAB)
        for tile in range(4):
            visit, half = 1 - tile // 2, tile % 2
            values = [v[:, tile * 128 : (tile + 1) * 128] for v in (cross, energy)]
            for kind in range(2):
                value = values[kind]
                if own == 0 and visit == 1:
                    value = jnp.where(m == 0, 0.0, value) + hr[1, kind, half]
                if own == GROUP - 1 and visit == 0:
                    value = value + hr[0, kind, half]
                rs[2 * own + half, kind, visit] = value

    def start_result(i, carry):
        result_copy(lax.rem(d + i, SUBS)).start()
        return carry

    def end_result(i, carry):
        result_arrival(lax.rem(d + i, SUBS)).wait()
        return carry

    lax.fori_loop(1, SUBS, start_result, 0)
    rr[d] = rs[d]
    lax.fori_loop(1, SUBS, end_result, 0)
    summed = rr[0]
    for sub in range(1, SUBS):
        summed = summed + rr[sub]
    score = summed[0] / jnp.sqrt(summed[1] / (CSPAN * TLEN) + EPS_ENERGY)
    for visit in range(2):
        o_ref[:, visit, :] = score[visit]


def shards(record, templates, offsets):
    ng = lax.axis_size("blk") // GROUP
    samples = record.shape[1]
    rows = CHUNK * ng
    buffer = (GROUP + 2) * SLAB
    wf, wi = transform_tables()
    vmem = pl.BlockSpec(memory_space=pltpu.VMEM)
    dma = pltpu.SemaphoreType.DMA
    return pl.pallas_call(
        functools.partial(kernel, ng),
        out_shape=jax.ShapeDtypeStruct((TD, 2, SLAB // 2), F32),
        in_specs=[vmem, vmem, pl.BlockSpec(memory_space=pltpu.SMEM), vmem, vmem],
        out_specs=vmem,
        scratch_shapes=[
            pltpu.VMEM((samples // FRAME * CHUNK, FRAME), F32),
            pltpu.VMEM((CHUNK, samples), BF16),
            pltpu.VMEM((rows // 32, 32, buffer), BF16),
            pltpu.VMEM((rows // 32, 32, buffer), BF16),
            pltpu.VMEM((SUBS, TD, 32, TLEN), BF16),
            pltpu.VMEM((SUBS, TD, 32, TLEN), BF16),
            pltpu.VMEM((2, 2, TD, 32, TLEN), BF16),
            pltpu.VMEM(((GROUP + 2) * TD, FOLD, 256), BF16),
            pltpu.VMEM((3 * SLAB, 2 * SLAB), BF16),
            pltpu.VMEM((GROUP + 2, TD, 128), jnp.int32),
            pltpu.SMEM((GROUP + 2, TD, 128), jnp.int32),
            pltpu.VMEM((GROUP + 2, TD, 8, 2 * SLAB), F32),
            pltpu.VMEM((GROUP + 2, TD, 8, 3 * SLAB), F32),
            pltpu.VMEM((2, 2, 2, TD, 128), F32),
            pltpu.VMEM((2, 2, 2, TD, 128), F32),
            pltpu.VMEM((SUBS, 2, 2, TD, 128), F32),
            pltpu.VMEM((SUBS, 2, 2, TD, 128), F32),
            dma((ng,)), dma((ng,)), dma((SUBS,)), dma((SUBS,)), dma((GROUP,)), dma((GROUP,)),
            dma((2,)), dma((2,)), dma((2,)), dma((2,)), dma((2,)), dma((2,)), dma((SUBS,)), dma((SUBS,)),
            dma((1,)),
        ],
        compiler_params=pltpu.CompilerParams(
            collective_id=0, has_side_effects=True, vmem_limit_bytes=48 * 2**20
        ),
    )(record, templates, offsets, jnp.asarray(wf), jnp.asarray(wi))


def solution(mesh):
    return jax.shard_map(
        shards,
        mesh=mesh,
        in_specs=(P(("blk", "ch"), None), P("blk", "ch", None), P("blk")),
        out_specs=P("blk", None, "ch"),
        check_vma=False,
    )
```

```python
import functools

import jax
import jax.numpy as jnp
import numpy as np
from jax import lax
from jax.experimental import pallas as pl
from jax.experimental.pallas import tpu as pltpu
from jax.sharding import PartitionSpec as P

MESH = pl.DeviceIdType.MESH
F32 = jnp.float32
BF16 = jnp.bfloat16

FRAME = 128
CHUNK = 16
CSPAN = 512
TLEN = 256
SLAB = 256
TD = 8
GROUP = 4
SUBS = 8
FOLD = 64
EPS_POWER = 1e-6
EPS_ENERGY = 1e-5


def transform_tables():
    n = np.arange(FRAME)
    col = np.arange(FRAME)
    freq = np.where(col <= 64, col, col - 64)
    angle = 2.0 * np.pi * ((n[:, None] * freq[None, :]) % FRAME) / FRAME
    basis = np.where(col <= 64, np.cos(angle), np.sin(angle))
    weight = np.where((col == 0) | (col == 64), 1.0, 2.0) / np.sqrt(FRAME)

    def split(table):
        high = table.astype(jnp.bfloat16)
        low = (table - high.astype(np.float64)).astype(jnp.bfloat16)
        top = np.concatenate([high, low], axis=1)
        bottom = np.concatenate([high, np.zeros_like(high)], axis=1)
        return np.concatenate([top, bottom], axis=0)

    return split(basis), split((basis * weight).T)


def split_rows(value):
    high = value.astype(BF16)
    low = (value - high.astype(F32)).astype(BF16)
    return jnp.concatenate([high, low], axis=1)


def left(value, count):
    return pltpu.roll(value, value.shape[1] - count, 1)


def kernel(
    ng, x_ref, t_ref, off_ref, wf_ref, wi_ref, o_ref,
    ys, ws, wz, wv, tsend, trecv, thalo, lhs, band, offv, offs, cb, qb, hs, hr, rs, rr,
    a_s, a_r, t_s, t_r, f_s, f_r, th_s, th_r, fh_s, fh_r, h_s, h_r, r_s, r_r, loc,
):
    b = lax.axis_index("blk")
    h = lax.axis_index("ch")
    m = lax.div(b, GROUP)
    e = lax.rem(b, GROUP)
    d = 2 * e + h
    up = lax.rem(m + 1, ng)
    down = lax.rem(m + ng - 1, ng)
    rows = CHUNK * ng
    frames = x_ref.shape[1] // FRAME
    wide = GROUP * SLAB

    def peer(sub):
        return {"blk": GROUP * m + lax.div(sub, 2), "ch": lax.rem(sub, 2)}

    def half_block(group):
        return pl.multiple_of(lax.rem(group, 2) * CHUNK, CHUNK)

    def far(group):
        return {"blk": GROUP * group + e}

    bar = pltpu.get_barrier_semaphore()

    def greet_peer(i, carry):
        pl.semaphore_signal(bar, inc=1, device_id=peer(lax.rem(d + i, SUBS)), device_id_type=MESH)
        return carry

    def greet_far(i, carry):
        pl.semaphore_signal(bar, inc=1, device_id=far(lax.rem(m + i, ng)), device_id_type=MESH)
        return carry

    lax.fori_loop(1, SUBS, greet_peer, 0)
    lax.fori_loop(1, ng, greet_far, 0)

    r_id = lax.broadcasted_iota(jnp.int32, (256, 256), 0)
    c_id = lax.broadcasted_iota(jnp.int32, (256, 256), 1)
    slot = 128 * ((r_id >> 4) & 1) + 16 * (r_id >> 5) + (r_id & 15)
    for k in range(TD):
        perm = jnp.where(((slot - c_id - off_ref[k]) & 255) == 0, 1.0, 0.0).astype(BF16)
        placed = jnp.dot(perm, t_ref[k], preferred_element_type=F32).astype(BF16)
        for s in range(SUBS):
            tsend[s, k] = placed[32 * s : 32 * s + 32]

    row8 = lax.broadcasted_iota(jnp.int32, (TD, 128), 0)
    own_off = jnp.zeros((TD, 128), jnp.int32)
    for k in range(TD):
        own_off = jnp.where(row8 == k, off_ref[k], own_off)
    offv[1 + e] = own_off

    pl.semaphore_wait(bar, SUBS - 1 + ng - 1)

    def template_copy(i):
        sub = lax.rem(d + i, SUBS)
        return pltpu.make_async_remote_copy(
            src_ref=tsend.at[sub], dst_ref=trecv.at[d], send_sem=t_s.at[sub], recv_sem=t_r.at[d],
            device_id=peer(sub), device_id_type=MESH,
        )

    def template_arrival(i):
        sub = lax.rem(d + i, SUBS)
        return pltpu.make_async_remote_copy(
            src_ref=tsend.at[sub], dst_ref=trecv.at[sub], send_sem=t_s.at[sub], recv_sem=t_r.at[sub],
            device_id=peer(sub), device_id_type=MESH,
        )

    def offset_copy(i):
        other = lax.rem(e + i, GROUP)
        return pltpu.make_async_remote_copy(
            src_ref=offv.at[1 + e], dst_ref=offv.at[1 + e], send_sem=f_s.at[other], recv_sem=f_r.at[e],
            device_id={"blk": GROUP * m + other}, device_id_type=MESH,
        )

    def offset_arrival(i):
        other = lax.rem(e + i, GROUP)
        return pltpu.make_async_remote_copy(
            src_ref=offv.at[1 + e], dst_ref=offv.at[1 + other], send_sem=f_s.at[other], recv_sem=f_r.at[other],
            device_id={"blk": GROUP * m + other}, device_id_type=MESH,
        )

    for i in range(1, GROUP):
        offset_copy(i).start()

    def start_template(i, carry):
        template_copy(i).start()
        return carry

    lax.fori_loop(1, SUBS, start_template, 0)

    step = 16
    wf = wf_ref[...]

    def forward(i, total):
        part = x_ref[:, pl.ds(pl.multiple_of(i * (step * FRAME), FRAME), step * FRAME)]
        stacked = jnp.concatenate([part[:, f * FRAME : (f + 1) * FRAME] for f in range(step)], axis=0)
        both = jnp.dot(split_rows(stacked), wf, preferred_element_type=F32)
        spec = both[:, :FRAME] + both[:, FRAME:]
        ys[pl.ds(pl.multiple_of(i * (step * CHUNK), 8), step * CHUNK), :] = spec
        return total + jnp.sum((spec * spec).reshape(step, CHUNK, FRAME), axis=0)

    total = lax.fori_loop(0, frames // step, forward, jnp.zeros((CHUNK, FRAME), F32), unroll=8)
    mean = total * (1.0 / frames)
    lane = lax.broadcasted_iota(jnp.int32, (CHUNK, FRAME), 1)
    power = jnp.where((lane & 63) == 0, mean, mean + pltpu.roll(mean, 64, 1))
    amp = 1.0 / jnp.sqrt(power + EPS_POWER)
    wi = wi_ref[...]

    def sample_copy(t):
        return pltpu.make_async_remote_copy(
            src_ref=ws.at[:, pl.ds(pl.multiple_of(t * wide, FRAME), wide)],
            dst_ref=wz.at[lax.div(m, 2), pl.ds(half_block(m), CHUNK), pl.ds(SLAB, wide)],
            send_sem=a_s.at[t], recv_sem=a_r.at[m], device_id=far(t), device_id_type=MESH,
        )

    def sample_arrival(t):
        return pltpu.make_async_remote_copy(
            src_ref=ws.at[:, pl.ds(pl.multiple_of(t * wide, FRAME), wide)],
            dst_ref=wz.at[lax.div(t, 2), pl.ds(half_block(t), CHUNK), pl.ds(SLAB, wide)],
            send_sem=a_s.at[t], recv_sem=a_r.at[t], device_id=far(t), device_id_type=MESH,
        )

    def back(i, carry):
        pair = lax.rem(lax.div(m, 2) + i, ng // 2)
        spec = ys[pl.ds(pl.multiple_of(pair * (step * CHUNK), 8), step * CHUNK), :]
        scaled = (spec.reshape(step, CHUNK, FRAME) * amp[None]).reshape(step * CHUNK, FRAME)
        both = jnp.dot(split_rows(scaled), wi, preferred_element_type=F32)
        white = (both[:, :FRAME] + both[:, FRAME:]).astype(BF16)
        for f in range(step):
            at = pl.multiple_of((pair * step + f) * FRAME, FRAME)
            ws[:, pl.ds(at, FRAME)] = white[f * CHUNK : (f + 1) * CHUNK]
        for q in range(2):
            t = 2 * pair + q

            @pl.when(t != m)
            def _():
                sample_copy(t).start()

        return carry

    lax.fori_loop(0, ng // 2, back, 0, unroll=8)

    wz[:, :, 0:SLAB] = jnp.zeros((rows // 32, 32, SLAB), BF16)
    wz[:, :, SLAB + wide : 2 * SLAB + wide] = jnp.zeros((rows // 32, 32, SLAB), BF16)
    wz[lax.div(m, 2), pl.ds(half_block(m), CHUNK), pl.ds(SLAB, wide)] = ws[
        :, pl.ds(pl.multiple_of(m * wide, FRAME), wide)
    ]
    trecv[d] = tsend[d]

    for i in range(1, GROUP):
        offset_arrival(i).wait()

    def end_template(i, carry):
        template_arrival(i).wait()
        return carry

    lax.fori_loop(1, SUBS, end_template, 0)

    def halo(side, kind):
        group = up if side == 0 else down
        first = SUBS - 2 if side == 0 else 0
        shard = GROUP if side == 0 else 1
        if kind == "t":
            src, dst, sems = trecv.at[pl.ds(first, 2)], thalo.at[side], (th_s, th_r)
        elif kind == "f":
            src, dst, sems = offv.at[shard], offv.at[(GROUP + 1) * side], (fh_s, fh_r)
        else:
            src, dst, sems = hs.at[side], hr.at[side], (h_s, h_r)
            group = down if side == 0 else up
        return pltpu.make_async_remote_copy(
            src_ref=src, dst_ref=dst, send_sem=sems[0].at[side], recv_sem=sems[1].at[side],
            device_id=far(group), device_id_type=MESH,
        )

    for side in range(2):
        halo(side, "f").start()
        halo(side, "t").start()

    w_id = lax.broadcasted_iota(jnp.int32, band.shape, 0)
    l_id = lax.broadcasted_iota(jnp.int32, band.shape, 1)
    gap = w_id - l_id
    band[...] = jnp.where((gap >= 0) & (gap < TLEN), 1.0, 0.0).astype(BF16)

    r_id = lax.broadcasted_iota(jnp.int32, (FOLD, TLEN), 0)
    s_id = lax.broadcasted_iota(jnp.int32, (FOLD, TLEN), 1)
    pick = jnp.where((s_id & (FOLD - 1)) == ((r_id & ~7) + 7 - (r_id & 7)), 1.0, 0.0).astype(BF16)
    part = lax.broadcasted_iota(jnp.int32, (2 * FOLD * 2, TLEN), 1) >> 6
    which = lax.broadcasted_iota(jnp.int32, (2 * FOLD * 2, TLEN), 0) >> 6
    keep = jnp.where(part == which, 1.0, 0.0).astype(BF16)

    def left_operand(first, second):
        both = jnp.concatenate([first, second], axis=0)
        spread = jnp.concatenate([both] * 4, axis=0) * keep
        turned = lax.dot_general(pick, spread, (((1,), (1,)), ((), ())), preferred_element_type=F32)
        return turned.astype(BF16)

    def prepare(q, carry):
        shard = lax.div(q, TD)
        k = lax.rem(q, TD)
        lhs[TD + q] = left_operand(trecv[2 * shard, k], trecv[2 * shard + 1, k])
        return carry

    lax.fori_loop(0, GROUP * TD, prepare, 0, unroll=8)

    for side in range(2):
        halo(side, "f").wait()
        halo(side, "t").wait()

    def prepare_halo(q, carry):
        side = lax.div(q, TD)
        k = lax.rem(q, TD)
        lhs[side * (GROUP + 1) * TD + k] = left_operand(thalo[side, 0, k], thalo[side, 1, k])
        return carry

    lax.fori_loop(0, 2 * TD, prepare_halo, 0, unroll=8)
    to_scalar = pltpu.make_async_copy(offv, offs, loc.at[0])
    to_scalar.start()
    to_scalar.wait()

    def shift_rows(t):
        at = pl.ds(half_block(t), CHUNK)
        block = wz[lax.div(t, 2), at, :]
        wv[lax.div(t, 2), at, :] = jnp.concatenate([block[:, FOLD:], block[:, :FOLD]], axis=1)

    shift_rows(m)

    def arrive(i, carry):
        t = lax.rem(m + i, ng)
        sample_arrival(t).wait()
        shift_rows(t)
        return carry

    lax.fori_loop(1, ng, arrive, 0)

    def correlate(shard, k, c0, width):
        off = offs[shard, k, 0]
        start = 16 * (off >> 7) + jnp.clip((off & 127) - 16 * d, 0, 16)
        r0 = start >> 5
        r1 = r0 + 1
        r2 = jnp.minimum(r0 + 2, rows // 32 - 1)
        late = lax.broadcasted_iota(jnp.int32, (32, width), 0) < (start & 31)
        cols = pl.ds(c0, width)

        def window(ref):
            b0, b1, b2 = ref[r0, :, cols], ref[r1, :, cols], ref[r2, :, cols]
            return jnp.concatenate([jnp.where(late, b1, b0), jnp.where(late, b2, b1)], axis=0)

        w = window(wz)
        v = window(wv)
        n = width - 128
        right = jnp.concatenate([w[:, :n], v[:, :n], w[:, 128:], v[:, 128:]], axis=0)
        prod = jnp.dot(lhs[shard * TD + k], right, preferred_element_type=F32)
        prod = prod[:32] + left(prod[32:], 32)
        prod = prod[:16] + left(prod[16:], 16)
        prod = prod[:8] + left(prod[8:], 8)
        prod = pltpu.roll(prod, n - 7, 1, stride=1, stride_axis=0)
        wide_w = w.astype(F32)
        return prod[:, : n - 128], jnp.sum((wide_w * wide_w).reshape(8, 8, width), axis=0)

    def window_energy(squares, width):
        high = squares.astype(BF16)
        rest = squares - high.astype(F32)
        mid = rest.astype(BF16)
        low = (rest - mid.astype(F32)).astype(BF16)
        sums = jnp.dot(
            jnp.concatenate([high, mid, low], axis=0), band[:width, : width - SLAB], preferred_element_type=F32
        )
        return sums[:TD] + sums[TD : 2 * TD] + sums[2 * TD :]

    for side in range(2):
        shard = (GROUP + 1) * side

        def edge(k, carry):
            cross, squares = correlate(shard, k, side * wide, 2 * SLAB)
            cb[shard, k, :, :SLAB] = cross
            qb[shard, k, :, : 2 * SLAB] = squares
            return carry

        lax.fori_loop(0, TD, edge, 0, unroll=8)
        cross = jnp.sum(cb[shard, :, :, :SLAB], axis=1)
        energy = window_energy(jnp.sum(qb[shard, :, :, : 2 * SLAB], axis=1), 2 * SLAB)
        if side == 0:
            cross = jnp.where(m == 0, 0.0, cross)
            energy = jnp.where(m == 0, 0.0, energy)
        for half in range(2):
            hs[side, 0, half] = cross[:, half * 128 : (half + 1) * 128]
            hs[side, 1, half] = energy[:, half * 128 : (half + 1) * 128]
        halo(side, "r").start()

    def inner(q, carry):
        shard = 1 + lax.div(q, TD)
        k = lax.rem(q, TD)
        cross, squares = correlate(shard, k, pl.multiple_of((shard - 1) * SLAB, SLAB), 3 * SLAB)
        cb[shard, k] = cross
        qb[shard, k] = squares
        return carry

    lax.fori_loop(0, GROUP * TD, inner, 0, unroll=8)

    def result_copy(sub):
        return pltpu.make_async_remote_copy(
            src_ref=rs.at[sub], dst_ref=rr.at[d], send_sem=r_s.at[sub], recv_sem=r_r.at[d],
            device_id=peer(sub), device_id_type=MESH,
        )

    def result_arrival(sub):
        return pltpu.make_async_remote_copy(
            src_ref=rs.at[sub], dst_ref=rr.at[sub], send_sem=r_s.at[sub], recv_sem=r_r.at[sub],
            device_id=peer(sub), device_id_type=MESH,
        )

    for side in range(2):
        halo(side, "r").wait()

    for own in range(GROUP):
        cross = jnp.sum(cb[1 + own], axis=1)
        energy = window_energy(jnp.sum(qb[1 + own], axis=1), 3 * SLAB)
        for tile in range(4):
            visit, half = 1 - tile // 2, tile % 2
            values = [v[:, tile * 128 : (tile + 1) * 128] for v in (cross, energy)]
            for kind in range(2):
                value = values[kind]
                if own == 0 and visit == 1:
                    value = jnp.where(m == 0, 0.0, value) + hr[1, kind, half]
                if own == GROUP - 1 and visit == 0:
                    value = value + hr[0, kind, half]
                rs[2 * own + half, kind, visit] = value

    def start_result(i, carry):
        result_copy(lax.rem(d + i, SUBS)).start()
        return carry

    def end_result(i, carry):
        result_arrival(lax.rem(d + i, SUBS)).wait()
        return carry

    lax.fori_loop(1, SUBS, start_result, 0)
    rr[d] = rs[d]
    lax.fori_loop(1, SUBS, end_result, 0)
    summed = rr[0]
    for sub in range(1, SUBS):
        summed = summed + rr[sub]
    score = summed[0] / jnp.sqrt(summed[1] / (CSPAN * TLEN) + EPS_ENERGY)
    for visit in range(2):
        o_ref[:, visit, :] = score[visit]


def shards(record, templates, offsets):
    ng = lax.axis_size("blk") // GROUP
    samples = record.shape[1]
    rows = CHUNK * ng
    buffer = (GROUP + 2) * SLAB
    wf, wi = transform_tables()
    vmem = pl.BlockSpec(memory_space=pltpu.VMEM)
    dma = pltpu.SemaphoreType.DMA
    return pl.pallas_call(
        functools.partial(kernel, ng),
        out_shape=jax.ShapeDtypeStruct((TD, 2, SLAB // 2), F32),
        in_specs=[vmem, vmem, pl.BlockSpec(memory_space=pltpu.SMEM), vmem, vmem],
        out_specs=vmem,
        scratch_shapes=[
            pltpu.VMEM((samples // FRAME * CHUNK, FRAME), F32),
            pltpu.VMEM((CHUNK, samples), BF16),
            pltpu.VMEM((rows // 32, 32, buffer), BF16),
            pltpu.VMEM((rows // 32, 32, buffer), BF16),
            pltpu.VMEM((SUBS, TD, 32, TLEN), BF16),
            pltpu.VMEM((SUBS, TD, 32, TLEN), BF16),
            pltpu.VMEM((2, 2, TD, 32, TLEN), BF16),
            pltpu.VMEM(((GROUP + 2) * TD, FOLD, 256), BF16),
            pltpu.VMEM((3 * SLAB, 2 * SLAB), BF16),
            pltpu.VMEM((GROUP + 2, TD, 128), jnp.int32),
            pltpu.SMEM((GROUP + 2, TD, 128), jnp.int32),
            pltpu.VMEM((GROUP + 2, TD, 8, 2 * SLAB), F32),
            pltpu.VMEM((GROUP + 2, TD, 8, 3 * SLAB), F32),
            pltpu.VMEM((2, 2, 2, TD, 128), F32),
            pltpu.VMEM((2, 2, 2, TD, 128), F32),
            pltpu.VMEM((SUBS, 2, 2, TD, 128), F32),
            pltpu.VMEM((SUBS, 2, 2, TD, 128), F32),
            dma((ng,)), dma((ng,)), dma((SUBS,)), dma((SUBS,)), dma((GROUP,)), dma((GROUP,)),
            dma((2,)), dma((2,)), dma((2,)), dma((2,)), dma((2,)), dma((2,)), dma((SUBS,)), dma((SUBS,)),
            dma((1,)),
        ],
        compiler_params=pltpu.CompilerParams(
            collective_id=0, has_side_effects=True, vmem_limit_bytes=48 * 2**20
        ),
    )(record, templates, offsets, jnp.asarray(wf), jnp.asarray(wi))


def solution(mesh):
    return jax.shard_map(
        shards,
        mesh=mesh,
        in_specs=(P(("blk", "ch"), None), P("blk", "ch", None), P("blk")),
        out_specs=P("blk", None, "ch"),
        check_vma=False,
    )
```

```python
import functools

import jax
import jax.numpy as jnp
import numpy as np
from jax import lax
from jax.experimental import pallas as pl
from jax.experimental.pallas import tpu as pltpu
from jax.sharding import PartitionSpec as P

MESH = pl.DeviceIdType.MESH
F32 = jnp.float32
BF16 = jnp.bfloat16

FRAME = 128
CHUNK = 16
CSPAN = 512
TLEN = 256
SLAB = 256
TD = 8
GROUP = 4
SUBS = 8
FOLD = 64
EPS_POWER = 1e-6
EPS_ENERGY = 1e-5


def transform_tables():
    n = np.arange(FRAME)
    col = np.arange(FRAME)
    freq = np.where(col <= 64, col, col - 64)
    angle = 2.0 * np.pi * ((n[:, None] * freq[None, :]) % FRAME) / FRAME
    basis = np.where(col <= 64, np.cos(angle), np.sin(angle))
    weight = np.where((col == 0) | (col == 64), 1.0, 2.0) / np.sqrt(FRAME)

    def split(table):
        high = table.astype(jnp.bfloat16)
        low = (table - high.astype(np.float64)).astype(jnp.bfloat16)
        top = np.concatenate([high, low], axis=1)
        bottom = np.concatenate([high, np.zeros_like(high)], axis=1)
        return np.concatenate([top, bottom], axis=0)

    return split(basis), split((basis * weight).T)


def split_rows(value):
    high = value.astype(BF16)
    low = (value - high.astype(F32)).astype(BF16)
    return jnp.concatenate([high, low], axis=1)


def left(value, count):
    return pltpu.roll(value, value.shape[1] - count, 1)


def kernel(
    ng, x_hbm, t_hbm, off_hbm, tab_hbm, o_ref,
    x_ref, t_ref, off_ref, tab_ref,
    ys, ws, wz, wv, tsend, trecv, thalo, lhs, band, offv, offs, cb, qb, hs, hr, rs, rr,
    a_s, a_r, t_s, t_r, f_s, f_r, th_s, th_r, fh_s, fh_r, h_s, h_r, r_s, r_r, loc, ld,
):
    b = lax.axis_index("blk")
    h = lax.axis_index("ch")
    m = lax.div(b, GROUP)
    e = lax.rem(b, GROUP)
    d = 2 * e + h
    up = lax.rem(m + 1, ng)
    down = lax.rem(m + ng - 1, ng)
    rows = CHUNK * ng
    frames = x_ref.shape[1] // FRAME
    wide = GROUP * SLAB

    def peer(sub):
        return {"blk": GROUP * m + lax.div(sub, 2), "ch": lax.rem(sub, 2)}

    def half_block(group):
        return pl.multiple_of(lax.rem(group, 2) * CHUNK, CHUNK)

    def far(group):
        return {"blk": GROUP * group + e}

    parts = 4
    span = x_ref.shape[1] // parts

    def load(i):
        if i < parts:
            cols = pl.ds(i * span, span)
            return pltpu.make_async_copy(x_hbm.at[:, cols], x_ref.at[:, cols], ld.at[i])
        src, dst = ((off_hbm, off_ref), (t_hbm, t_ref), (tab_hbm, tab_ref))[i - parts]
        return pltpu.make_async_copy(src, dst, ld.at[i])

    for i in (parts, parts + 1, parts + 2, *range(parts)):
        load(i).start()

    bar = pltpu.get_barrier_semaphore()

    def greet_peer(i, carry):
        pl.semaphore_signal(bar, inc=1, device_id=peer(lax.rem(d + i, SUBS)), device_id_type=MESH)
        return carry

    def greet_far(i, carry):
        pl.semaphore_signal(bar, inc=1, device_id=far(lax.rem(m + i, ng)), device_id_type=MESH)
        return carry

    lax.fori_loop(1, SUBS, greet_peer, 0)
    lax.fori_loop(1, ng, greet_far, 0)

    r_id = lax.broadcasted_iota(jnp.int32, (256, 256), 0)
    c_id = lax.broadcasted_iota(jnp.int32, (256, 256), 1)
    slot = 128 * ((r_id >> 4) & 1) + 16 * (r_id >> 5) + (r_id & 15)
    load(parts).wait()
    load(parts + 1).wait()
    for k in range(TD):
        perm = jnp.where(((slot - c_id - off_ref[k]) & 255) == 0, 1.0, 0.0).astype(BF16)
        placed = jnp.dot(perm, t_ref[k], preferred_element_type=F32).astype(BF16)
        for s in range(SUBS):
            tsend[s, k] = placed[32 * s : 32 * s + 32]

    row8 = lax.broadcasted_iota(jnp.int32, (TD, 128), 0)
    own_off = jnp.zeros((TD, 128), jnp.int32)
    for k in range(TD):
        own_off = jnp.where(row8 == k, off_ref[k], own_off)
    offv[1 + e] = own_off

    pl.semaphore_wait(bar, SUBS - 1 + ng - 1)

    def template_copy(i):
        sub = lax.rem(d + i, SUBS)
        return pltpu.make_async_remote_copy(
            src_ref=tsend.at[sub], dst_ref=trecv.at[d], send_sem=t_s.at[sub], recv_sem=t_r.at[d],
            device_id=peer(sub), device_id_type=MESH,
        )

    def template_arrival(i):
        sub = lax.rem(d + i, SUBS)
        return pltpu.make_async_remote_copy(
            src_ref=tsend.at[sub], dst_ref=trecv.at[sub], send_sem=t_s.at[sub], recv_sem=t_r.at[sub],
            device_id=peer(sub), device_id_type=MESH,
        )

    def offset_copy(i):
        other = lax.rem(e + i, GROUP)
        return pltpu.make_async_remote_copy(
            src_ref=offv.at[1 + e], dst_ref=offv.at[1 + e], send_sem=f_s.at[other], recv_sem=f_r.at[e],
            device_id={"blk": GROUP * m + other}, device_id_type=MESH,
        )

    def offset_arrival(i):
        other = lax.rem(e + i, GROUP)
        return pltpu.make_async_remote_copy(
            src_ref=offv.at[1 + e], dst_ref=offv.at[1 + other], send_sem=f_s.at[other], recv_sem=f_r.at[other],
            device_id={"blk": GROUP * m + other}, device_id_type=MESH,
        )

    for i in range(1, GROUP):
        offset_copy(i).start()

    def start_template(i, carry):
        template_copy(i).start()
        return carry

    lax.fori_loop(1, SUBS, start_template, 0)

    step = 16
    load(parts + 2).wait()
    wf = tab_ref[0]

    def forward(i, total):
        part = x_ref[:, pl.ds(pl.multiple_of(i * (step * FRAME), FRAME), step * FRAME)]
        stacked = jnp.concatenate([part[:, f * FRAME : (f + 1) * FRAME] for f in range(step)], axis=0)
        both = jnp.dot(split_rows(stacked), wf, preferred_element_type=F32)
        spec = both[:, :FRAME] + both[:, FRAME:]
        ys[pl.ds(pl.multiple_of(i * (step * CHUNK), 8), step * CHUNK), :] = spec
        return total + jnp.sum((spec * spec).reshape(step, CHUNK, FRAME), axis=0)

    total = jnp.zeros((CHUNK, FRAME), F32)
    turns = frames // step // parts
    for i in range(parts):
        load(i).wait()
        total = lax.fori_loop(i * turns, (i + 1) * turns, forward, total, unroll=4)
    mean = total * (1.0 / frames)
    lane = lax.broadcasted_iota(jnp.int32, (CHUNK, FRAME), 1)
    power = jnp.where((lane & 63) == 0, mean, mean + pltpu.roll(mean, 64, 1))
    amp = 1.0 / jnp.sqrt(power + EPS_POWER)
    wi = tab_ref[1]

    def sample_copy(t):
        return pltpu.make_async_remote_copy(
            src_ref=ws.at[:, pl.ds(pl.multiple_of(t * wide, FRAME), wide)],
            dst_ref=wz.at[lax.div(m, 2), pl.ds(half_block(m), CHUNK), pl.ds(SLAB, wide)],
            send_sem=a_s.at[t], recv_sem=a_r.at[m], device_id=far(t), device_id_type=MESH,
        )

    def sample_arrival(t):
        return pltpu.make_async_remote_copy(
            src_ref=ws.at[:, pl.ds(pl.multiple_of(t * wide, FRAME), wide)],
            dst_ref=wz.at[lax.div(t, 2), pl.ds(half_block(t), CHUNK), pl.ds(SLAB, wide)],
            send_sem=a_s.at[t], recv_sem=a_r.at[t], device_id=far(t), device_id_type=MESH,
        )

    def back(i, carry):
        pair = lax.rem(lax.div(m, 2) + i, ng // 2)
        spec = ys[pl.ds(pl.multiple_of(pair * (step * CHUNK), 8), step * CHUNK), :]
        scaled = (spec.reshape(step, CHUNK, FRAME) * amp[None]).reshape(step * CHUNK, FRAME)
        both = jnp.dot(split_rows(scaled), wi, preferred_element_type=F32)
        white = (both[:, :FRAME] + both[:, FRAME:]).astype(BF16)
        for f in range(step):
            at = pl.multiple_of((pair * step + f) * FRAME, FRAME)
            ws[:, pl.ds(at, FRAME)] = white[f * CHUNK : (f + 1) * CHUNK]
        for q in range(2):
            t = 2 * pair + q

            @pl.when(t != m)
            def _():
                sample_copy(t).start()

        return carry

    lax.fori_loop(0, ng // 2, back, 0, unroll=8)

    wz[:, :, 0:SLAB] = jnp.zeros((rows // 32, 32, SLAB), BF16)
    wz[:, :, SLAB + wide : 2 * SLAB + wide] = jnp.zeros((rows // 32, 32, SLAB), BF16)
    wz[lax.div(m, 2), pl.ds(half_block(m), CHUNK), pl.ds(SLAB, wide)] = ws[
        :, pl.ds(pl.multiple_of(m * wide, FRAME), wide)
    ]
    trecv[d] = tsend[d]

    for i in range(1, GROUP):
        offset_arrival(i).wait()

    def end_template(i, carry):
        template_arrival(i).wait()
        return carry

    lax.fori_loop(1, SUBS, end_template, 0)

    def halo(side, kind):
        group = up if side == 0 else down
        first = SUBS - 2 if side == 0 else 0
        shard = GROUP if side == 0 else 1
        if kind == "t":
            src, dst, sems = trecv.at[pl.ds(first, 2)], thalo.at[side], (th_s, th_r)
        elif kind == "f":
            src, dst, sems = offv.at[shard], offv.at[(GROUP + 1) * side], (fh_s, fh_r)
        else:
            src, dst, sems = hs.at[side], hr.at[side], (h_s, h_r)
            group = down if side == 0 else up
        return pltpu.make_async_remote_copy(
            src_ref=src, dst_ref=dst, send_sem=sems[0].at[side], recv_sem=sems[1].at[side],
            device_id=far(group), device_id_type=MESH,
        )

    for side in range(2):
        halo(side, "f").start()
        halo(side, "t").start()

    w_id = lax.broadcasted_iota(jnp.int32, band.shape, 0)
    l_id = lax.broadcasted_iota(jnp.int32, band.shape, 1)
    gap = w_id - l_id
    band[...] = jnp.where((gap >= 0) & (gap < TLEN), 1.0, 0.0).astype(BF16)

    r_id = lax.broadcasted_iota(jnp.int32, (FOLD, TLEN), 0)
    s_id = lax.broadcasted_iota(jnp.int32, (FOLD, TLEN), 1)
    pick = jnp.where((s_id & (FOLD - 1)) == ((r_id & ~7) + 7 - (r_id & 7)), 1.0, 0.0).astype(BF16)
    part = lax.broadcasted_iota(jnp.int32, (2 * FOLD * 2, TLEN), 1) >> 6
    which = lax.broadcasted_iota(jnp.int32, (2 * FOLD * 2, TLEN), 0) >> 6
    keep = jnp.where(part == which, 1.0, 0.0).astype(BF16)

    def left_operand(first, second):
        both = jnp.concatenate([first, second], axis=0)
        spread = jnp.concatenate([both] * 4, axis=0) * keep
        turned = lax.dot_general(pick, spread, (((1,), (1,)), ((), ())), preferred_element_type=F32)
        return turned.astype(BF16)

    def prepare(q, carry):
        shard = lax.div(q, TD)
        k = lax.rem(q, TD)
        lhs[TD + q] = left_operand(trecv[2 * shard, k], trecv[2 * shard + 1, k])
        return carry

    lax.fori_loop(0, GROUP * TD, prepare, 0, unroll=8)

    for side in range(2):
        halo(side, "f").wait()
        halo(side, "t").wait()

    def prepare_halo(q, carry):
        side = lax.div(q, TD)
        k = lax.rem(q, TD)
        lhs[side * (GROUP + 1) * TD + k] = left_operand(thalo[side, 0, k], thalo[side, 1, k])
        return carry

    lax.fori_loop(0, 2 * TD, prepare_halo, 0, unroll=8)
    to_scalar = pltpu.make_async_copy(offv, offs, loc.at[0])
    to_scalar.start()
    to_scalar.wait()

    def shift_rows(t):
        at = pl.ds(half_block(t), CHUNK)
        block = wz[lax.div(t, 2), at, :]
        wv[lax.div(t, 2), at, :] = jnp.concatenate([block[:, FOLD:], block[:, :FOLD]], axis=1)

    shift_rows(m)

    def arrive(i, carry):
        t = lax.rem(m + i, ng)
        sample_arrival(t).wait()
        shift_rows(t)
        return carry

    lax.fori_loop(1, ng, arrive, 0)

    def correlate(shard, k, c0, width):
        off = offs[shard, k, 0]
        start = 16 * (off >> 7) + jnp.clip((off & 127) - 16 * d, 0, 16)
        r0 = start >> 5
        r1 = r0 + 1
        r2 = jnp.minimum(r0 + 2, rows // 32 - 1)
        late = lax.broadcasted_iota(jnp.int32, (32, width), 0) < (start & 31)
        cols = pl.ds(c0, width)

        def window(ref):
            b0, b1, b2 = ref[r0, :, cols], ref[r1, :, cols], ref[r2, :, cols]
            return jnp.concatenate([jnp.where(late, b1, b0), jnp.where(late, b2, b1)], axis=0)

        w = window(wz)
        v = window(wv)
        n = width - 128
        right = jnp.concatenate([w[:, :n], v[:, :n], w[:, 128:], v[:, 128:]], axis=0)
        prod = jnp.dot(lhs[shard * TD + k], right, preferred_element_type=F32)
        prod = prod[:32] + left(prod[32:], 32)
        prod = prod[:16] + left(prod[16:], 16)
        prod = prod[:8] + left(prod[8:], 8)
        prod = pltpu.roll(prod, n - 7, 1, stride=1, stride_axis=0)
        wide_w = w.astype(F32)
        return prod[:, : n - 128], jnp.sum((wide_w * wide_w).reshape(8, 8, width), axis=0)

    def window_energy(squares, width):
        high = squares.astype(BF16)
        rest = squares - high.astype(F32)
        mid = rest.astype(BF16)
        low = (rest - mid.astype(F32)).astype(BF16)
        sums = jnp.dot(
            jnp.concatenate([high, mid, low], axis=0), band[:width, : width - SLAB], preferred_element_type=F32
        )
        return sums[:TD] + sums[TD : 2 * TD] + sums[2 * TD :]

    for side in range(2):
        shard = (GROUP + 1) * side

        def edge(k, carry):
            cross, squares = correlate(shard, k, side * wide, 2 * SLAB)
            cb[shard, k, :, :SLAB] = cross
            qb[shard, k, :, : 2 * SLAB] = squares
            return carry

        lax.fori_loop(0, TD, edge, 0, unroll=8)
        cross = jnp.sum(cb[shard, :, :, :SLAB], axis=1)
        energy = window_energy(jnp.sum(qb[shard, :, :, : 2 * SLAB], axis=1), 2 * SLAB)
        if side == 0:
            cross = jnp.where(m == 0, 0.0, cross)
            energy = jnp.where(m == 0, 0.0, energy)
        for half in range(2):
            hs[side, 0, half] = cross[:, half * 128 : (half + 1) * 128]
            hs[side, 1, half] = energy[:, half * 128 : (half + 1) * 128]
        halo(side, "r").start()

    def inner(q, carry):
        shard = 1 + lax.div(q, TD)
        k = lax.rem(q, TD)
        cross, squares = correlate(shard, k, pl.multiple_of((shard - 1) * SLAB, SLAB), 3 * SLAB)
        cb[shard, k] = cross
        qb[shard, k] = squares
        return carry

    lax.fori_loop(0, GROUP * TD, inner, 0, unroll=8)

    def result_copy(sub):
        return pltpu.make_async_remote_copy(
            src_ref=rs.at[sub], dst_ref=rr.at[d], send_sem=r_s.at[sub], recv_sem=r_r.at[d],
            device_id=peer(sub), device_id_type=MESH,
        )

    def result_arrival(sub):
        return pltpu.make_async_remote_copy(
            src_ref=rs.at[sub], dst_ref=rr.at[sub], send_sem=r_s.at[sub], recv_sem=r_r.at[sub],
            device_id=peer(sub), device_id_type=MESH,
        )

    for side in range(2):
        halo(side, "r").wait()

    for own in range(GROUP):
        cross = jnp.sum(cb[1 + own], axis=1)
        energy = window_energy(jnp.sum(qb[1 + own], axis=1), 3 * SLAB)
        for tile in range(4):
            visit, half = 1 - tile // 2, tile % 2
            values = [v[:, tile * 128 : (tile + 1) * 128] for v in (cross, energy)]
            for kind in range(2):
                value = values[kind]
                if own == 0 and visit == 1:
                    value = jnp.where(m == 0, 0.0, value) + hr[1, kind, half]
                if own == GROUP - 1 and visit == 0:
                    value = value + hr[0, kind, half]
                rs[2 * own + half, kind, visit] = value

    def start_result(i, carry):
        result_copy(lax.rem(d + i, SUBS)).start()
        return carry

    def end_result(i, carry):
        result_arrival(lax.rem(d + i, SUBS)).wait()
        return carry

    lax.fori_loop(1, SUBS, start_result, 0)
    rr[d] = rs[d]
    lax.fori_loop(1, SUBS, end_result, 0)
    summed = rr[0]
    for sub in range(1, SUBS):
        summed = summed + rr[sub]
    score = summed[0] / jnp.sqrt(summed[1] / (CSPAN * TLEN) + EPS_ENERGY)
    for visit in range(2):
        o_ref[:, visit, :] = score[visit]


def shards(record, templates, offsets):
    ng = lax.axis_size("blk") // GROUP
    samples = record.shape[1]
    rows = CHUNK * ng
    buffer = (GROUP + 2) * SLAB
    tables = jnp.asarray(np.stack(transform_tables()))
    hbm = pl.BlockSpec(memory_space=pl.ANY)
    dma = pltpu.SemaphoreType.DMA
    return pl.pallas_call(
        functools.partial(kernel, ng),
        out_shape=jax.ShapeDtypeStruct((TD, 2, SLAB // 2), F32),
        in_specs=[hbm, hbm, hbm, hbm],
        out_specs=pl.BlockSpec(memory_space=pltpu.VMEM),
        scratch_shapes=[
            pltpu.VMEM(record.shape, F32),
            pltpu.VMEM(templates.shape, BF16),
            pltpu.SMEM(offsets.shape, jnp.int32),
            pltpu.VMEM(tables.shape, BF16),
            pltpu.VMEM((samples // FRAME * CHUNK, FRAME), F32),
            pltpu.VMEM((CHUNK, samples), BF16),
            pltpu.VMEM((rows // 32, 32, buffer), BF16),
            pltpu.VMEM((rows // 32, 32, buffer), BF16),
            pltpu.VMEM((SUBS, TD, 32, TLEN), BF16),
            pltpu.VMEM((SUBS, TD, 32, TLEN), BF16),
            pltpu.VMEM((2, 2, TD, 32, TLEN), BF16),
            pltpu.VMEM(((GROUP + 2) * TD, FOLD, 256), BF16),
            pltpu.VMEM((3 * SLAB, 2 * SLAB), BF16),
            pltpu.VMEM((GROUP + 2, TD, 128), jnp.int32),
            pltpu.SMEM((GROUP + 2, TD, 128), jnp.int32),
            pltpu.VMEM((GROUP + 2, TD, 8, 2 * SLAB), F32),
            pltpu.VMEM((GROUP + 2, TD, 8, 3 * SLAB), F32),
            pltpu.VMEM((2, 2, 2, TD, 128), F32),
            pltpu.VMEM((2, 2, 2, TD, 128), F32),
            pltpu.VMEM((SUBS, 2, 2, TD, 128), F32),
            pltpu.VMEM((SUBS, 2, 2, TD, 128), F32),
            dma((ng,)), dma((ng,)), dma((SUBS,)), dma((SUBS,)), dma((GROUP,)), dma((GROUP,)),
            dma((2,)), dma((2,)), dma((2,)), dma((2,)), dma((2,)), dma((2,)), dma((SUBS,)), dma((SUBS,)),
            dma((1,)), dma((7,)),
        ],
        compiler_params=pltpu.CompilerParams(
            collective_id=0, has_side_effects=True, vmem_limit_bytes=60 * 2**20
        ),
    )(record, templates, offsets, tables)


def solution(mesh):
    return jax.shard_map(
        shards,
        mesh=mesh,
        in_specs=(P(("blk", "ch"), None), P("blk", "ch", None), P("blk")),
        out_specs=P("blk", None, "ch"),
        check_vma=False,
    )
```

```python
import functools

import jax
import jax.numpy as jnp
import numpy as np
from jax import lax
from jax.experimental import pallas as pl
from jax.experimental.pallas import tpu as pltpu
from jax.sharding import PartitionSpec as P

MESH = pl.DeviceIdType.MESH
F32 = jnp.float32
BF16 = jnp.bfloat16

FRAME = 128
CHUNK = 16
CSPAN = 512
TLEN = 256
SLAB = 256
TD = 8
GROUP = 4
SUBS = 8
FOLD = 64
EPS_POWER = 1e-6
EPS_ENERGY = 1e-5


def transform_tables():
    n = np.arange(FRAME)
    col = np.arange(FRAME)
    freq = np.where(col <= 64, col, col - 64)
    angle = 2.0 * np.pi * ((n[:, None] * freq[None, :]) % FRAME) / FRAME
    basis = np.where(col <= 64, np.cos(angle), np.sin(angle))
    weight = np.where((col == 0) | (col == 64), 1.0, 2.0) / np.sqrt(FRAME)

    return np.stack([basis, (basis * weight).T]).astype(np.float32)


def split_table(table):
    high = table.astype(BF16)
    low = (table - high.astype(F32)).astype(BF16)
    top = jnp.concatenate([high, low], axis=1)
    bottom = jnp.concatenate([high, jnp.zeros_like(high)], axis=1)
    return jnp.concatenate([top, bottom], axis=0)


def split_rows(value):
    high = value.astype(BF16)
    low = (value - high.astype(F32)).astype(BF16)
    return jnp.concatenate([high, low], axis=1)


def left(value, count):
    return pltpu.roll(value, value.shape[1] - count, 1)


def kernel(
    ng, x_hbm, t_hbm, off_hbm, tab_hbm, o_ref,
    x_ref, t_ref, off_ref, tab_ref,
    ys, ws, land, wz, wv, tsend, trecv, thalo, lhs, band, offv, offs, cb, qb, hs, hr, rs, rr,
    a_s, a_r, t_s, t_r, f_s, f_r, th_s, th_r, fh_s, fh_r, h_s, h_r, r_s, r_r, loc, ld,
):
    b = lax.axis_index("blk")
    h = lax.axis_index("ch")
    m = lax.div(b, GROUP)
    e = lax.rem(b, GROUP)
    d = 2 * e + h
    up = lax.rem(m + 1, ng)
    down = lax.rem(m + ng - 1, ng)
    rows = CHUNK * ng
    frames = x_ref.shape[1] // FRAME
    wide = GROUP * SLAB

    def peer(sub):
        return {"blk": GROUP * m + lax.div(sub, 2), "ch": lax.rem(sub, 2)}

    def half_block(group):
        return pl.multiple_of(lax.rem(group, 2) * CHUNK, CHUNK)

    def far(group):
        return {"blk": GROUP * group + e}

    parts = 4
    span = x_ref.shape[1] // parts

    def load(i):
        if i < parts:
            cols = pl.ds(i * span, span)
            return pltpu.make_async_copy(x_hbm.at[:, cols], x_ref.at[:, cols], ld.at[i])
        src, dst = ((off_hbm, off_ref), (t_hbm, t_ref), (tab_hbm, tab_ref))[i - parts]
        return pltpu.make_async_copy(src, dst, ld.at[i])

    for i in (parts, parts + 1, parts + 2, *range(parts)):
        load(i).start()

    bar = pltpu.get_barrier_semaphore()

    def greet_peer(i, carry):
        pl.semaphore_signal(bar, inc=1, device_id=peer(lax.rem(d + i, SUBS)), device_id_type=MESH)
        return carry

    def greet_far(i, carry):
        pl.semaphore_signal(bar, inc=1, device_id=far(lax.rem(m + i, ng)), device_id_type=MESH)
        return carry

    lax.fori_loop(1, SUBS, greet_peer, 0)
    lax.fori_loop(1, ng, greet_far, 0)

    r_id = lax.broadcasted_iota(jnp.int32, (256, 256), 0)
    c_id = lax.broadcasted_iota(jnp.int32, (256, 256), 1)
    slot = 128 * ((r_id >> 4) & 1) + 16 * (r_id >> 5) + (r_id & 15)
    load(parts).wait()
    load(parts + 1).wait()
    for k in range(TD):
        perm = jnp.where(((slot - c_id - off_ref[k]) & 255) == 0, 1.0, 0.0).astype(BF16)
        placed = jnp.dot(perm, t_ref[k], preferred_element_type=F32).astype(BF16)
        for s in range(SUBS):
            tsend[s, k] = placed[32 * s : 32 * s + 32]

    row8 = lax.broadcasted_iota(jnp.int32, (TD, 128), 0)
    own_off = jnp.zeros((TD, 128), jnp.int32)
    for k in range(TD):
        own_off = jnp.where(row8 == k, off_ref[k], own_off)
    offv[1 + e] = own_off

    pl.semaphore_wait(bar, SUBS - 1 + ng - 1)

    def template_copy(i):
        sub = lax.rem(d + i, SUBS)
        return pltpu.make_async_remote_copy(
            src_ref=tsend.at[sub], dst_ref=trecv.at[d], send_sem=t_s.at[sub], recv_sem=t_r.at[d],
            device_id=peer(sub), device_id_type=MESH,
        )

    def template_arrival(i):
        sub = lax.rem(d + i, SUBS)
        return pltpu.make_async_remote_copy(
            src_ref=tsend.at[sub], dst_ref=trecv.at[sub], send_sem=t_s.at[sub], recv_sem=t_r.at[sub],
            device_id=peer(sub), device_id_type=MESH,
        )

    def offset_copy(i):
        other = lax.rem(e + i, GROUP)
        return pltpu.make_async_remote_copy(
            src_ref=offv.at[1 + e], dst_ref=offv.at[1 + e], send_sem=f_s.at[other], recv_sem=f_r.at[e],
            device_id={"blk": GROUP * m + other}, device_id_type=MESH,
        )

    def offset_arrival(i):
        other = lax.rem(e + i, GROUP)
        return pltpu.make_async_remote_copy(
            src_ref=offv.at[1 + e], dst_ref=offv.at[1 + other], send_sem=f_s.at[other], recv_sem=f_r.at[other],
            device_id={"blk": GROUP * m + other}, device_id_type=MESH,
        )

    for i in range(1, GROUP):
        offset_copy(i).start()

    def start_template(i, carry):
        template_copy(i).start()
        return carry

    lax.fori_loop(1, SUBS, start_template, 0)

    step = 16
    load(parts + 2).wait()
    wf = split_table(tab_ref[0])

    def forward(i, total):
        part = x_ref[:, pl.ds(pl.multiple_of(i * (step * FRAME), FRAME), step * FRAME)]
        stacked = jnp.concatenate([part[:, f * FRAME : (f + 1) * FRAME] for f in range(step)], axis=0)
        both = jnp.dot(split_rows(stacked), wf, preferred_element_type=F32)
        spec = both[:, :FRAME] + both[:, FRAME:]
        ys[pl.ds(pl.multiple_of(i * (step * CHUNK), 8), step * CHUNK), :] = spec
        return total + jnp.sum((spec * spec).reshape(step, CHUNK, FRAME), axis=0)

    total = jnp.zeros((CHUNK, FRAME), F32)
    turns = frames // step // parts
    for i in range(parts):
        load(i).wait()
        total = lax.fori_loop(i * turns, (i + 1) * turns, forward, total, unroll=4)
    mean = total * (1.0 / frames)
    lane = lax.broadcasted_iota(jnp.int32, (CHUNK, FRAME), 1)
    power = jnp.where((lane & 63) == 0, mean, mean + pltpu.roll(mean, 64, 1))
    amp = 1.0 / jnp.sqrt(power + EPS_POWER)
    wi = split_table(tab_ref[1])

    def sample_copy(t, wave, source):
        cols = 2 * SLAB * wave
        return pltpu.make_async_remote_copy(
            src_ref=ws.at[:, pl.ds(pl.multiple_of(t * wide + cols, FRAME), 2 * SLAB)],
            dst_ref=land.at[wave, source],
            send_sem=a_s.at[wave, t], recv_sem=a_r.at[wave, source], device_id=far(t), device_id_type=MESH,
        )

    def back(wave):
        def turn(i, carry):
            quad = lax.rem(lax.div(m, 4) + i, ng // 4)
            spec = []
            for q in range(4):
                base = (4 * quad + q) * (8 * CHUNK)
                for first, count in (((0, 2), (6, 2)), ((2, 4),))[wave]:
                    spec.append(ys[pl.ds(pl.multiple_of(base + first * CHUNK, 8), count * CHUNK), :])
            spec = jnp.concatenate(spec, axis=0)
            scaled = (spec.reshape(step, CHUNK, FRAME) * amp[None]).reshape(step * CHUNK, FRAME)
            both = jnp.dot(split_rows(scaled), wi, preferred_element_type=F32)
            white = (both[:, :FRAME] + both[:, FRAME:]).astype(BF16)
            for f in range(step):
                at = (4 * quad + f // 4) * wide + 2 * SLAB * wave + (f % 4) * FRAME
                ws[:, pl.ds(pl.multiple_of(at, FRAME), FRAME)] = white[f * CHUNK : (f + 1) * CHUNK]
            for q in range(4):
                t = 4 * quad + q

                @pl.when(t != m)
                def _():
                    sample_copy(t, wave, m).start()

            return carry

        lax.fori_loop(0, ng // 4, turn, 0, unroll=4)
        land[wave, m] = ws[
            :, pl.ds(pl.multiple_of(m * wide + 2 * SLAB * wave, FRAME), 2 * SLAB)
        ]

    back(0)

    wz[:, :, 0:SLAB] = jnp.zeros((rows // 32, 32, SLAB), BF16)
    wz[:, :, 5 * SLAB : 6 * SLAB] = jnp.zeros((rows // 32, 32, SLAB), BF16)
    wv[:, :, 5 * SLAB : 6 * SLAB] = jnp.zeros((rows // 32, 32, SLAB), BF16)
    trecv[d] = tsend[d]

    for i in range(1, GROUP):
        offset_arrival(i).wait()

    def end_template(i, carry):
        template_arrival(i).wait()
        return carry

    lax.fori_loop(1, SUBS, end_template, 0)

    def halo(side, kind):
        group = up if side == 0 else down
        first = SUBS - 2 if side == 0 else 0
        shard = GROUP if side == 0 else 1
        if kind == "t":
            src, dst, sems = trecv.at[pl.ds(first, 2)], thalo.at[side], (th_s, th_r)
        elif kind == "f":
            src, dst, sems = offv.at[shard], offv.at[(GROUP + 1) * side], (fh_s, fh_r)
        else:
            src, dst, sems = hs.at[side], hr.at[side], (h_s, h_r)
            group = down if side == 0 else up
        return pltpu.make_async_remote_copy(
            src_ref=src, dst_ref=dst, send_sem=sems[0].at[side], recv_sem=sems[1].at[side],
            device_id=far(group), device_id_type=MESH,
        )

    for side in range(2):
        halo(side, "f").start()
        halo(side, "t").start()

    back(1)

    w_id = lax.broadcasted_iota(jnp.int32, band.shape, 0)
    l_id = lax.broadcasted_iota(jnp.int32, band.shape, 1)
    gap = w_id - l_id
    band[...] = jnp.where((gap >= 0) & (gap < TLEN), 1.0, 0.0).astype(BF16)

    r_id = lax.broadcasted_iota(jnp.int32, (FOLD, TLEN), 0)
    s_id = lax.broadcasted_iota(jnp.int32, (FOLD, TLEN), 1)
    pick = jnp.where((s_id & (FOLD - 1)) == ((r_id & ~7) + 7 - (r_id & 7)), 1.0, 0.0).astype(BF16)
    part = lax.broadcasted_iota(jnp.int32, (2 * FOLD * 2, TLEN), 1) >> 6
    which = lax.broadcasted_iota(jnp.int32, (2 * FOLD * 2, TLEN), 0) >> 6
    keep = jnp.where(part == which, 1.0, 0.0).astype(BF16)

    def left_operand(first, second):
        both = jnp.concatenate([first, second], axis=0)
        spread = jnp.concatenate([both] * 4, axis=0) * keep
        turned = lax.dot_general(pick, spread, (((1,), (1,)), ((), ())), preferred_element_type=F32)
        return turned.astype(BF16)

    def prepare(q, carry):
        shard = lax.div(q, TD)
        k = lax.rem(q, TD)
        lhs[TD + q] = left_operand(trecv[2 * shard, k], trecv[2 * shard + 1, k])
        return carry

    lax.fori_loop(0, GROUP * TD, prepare, 0, unroll=8)

    for side in range(2):
        halo(side, "f").wait()
        halo(side, "t").wait()

    def prepare_halo(q, carry):
        side = lax.div(q, TD)
        k = lax.rem(q, TD)
        lhs[side * (GROUP + 1) * TD + k] = left_operand(thalo[side, 0, k], thalo[side, 1, k])
        return carry

    lax.fori_loop(0, 2 * TD, prepare_halo, 0, unroll=8)
    to_scalar = pltpu.make_async_copy(offv, offs, loc.at[0])
    to_scalar.start()
    to_scalar.wait()

    def shift_slabs(t, wave):
        at = pl.ds(half_block(t), CHUNK)
        row = lax.div(t, 2)

        block = land[wave, t]
        new = 1 + 2 * wave
        wz[row, at, new * SLAB : (new + 2) * SLAB] = block
        one, two = block[:, :SLAB], block[:, SLAB:]

        def put(i, block, after):
            wv[row, at, i * SLAB : (i + 1) * SLAB] = jnp.concatenate([block[:, FOLD:], after[:, :FOLD]], axis=1)

        none = jnp.zeros((CHUNK, SLAB), BF16)
        if wave == 0:
            put(0, none, one)
            put(1, one, none)
            put(2, two, none)
        else:
            put(1, wz[row, at, SLAB : 2 * SLAB], one)
            put(3, one, two)
            put(4, two, wz[row, at, 2 * SLAB : 3 * SLAB])

    def arrivals(wave):
        def arrive(i, carry):
            t = lax.rem(m + i, ng)
            sample_copy(t, wave, t).wait()
            shift_slabs(t, wave)
            return carry

        shift_slabs(m, wave)
        lax.fori_loop(1, ng, arrive, 0)

    def correlate(shard, k, slabs):
        off = offs[shard, k, 0]
        start = 16 * (off >> 7) + jnp.clip((off & 127) - 16 * d, 0, 16)
        r0 = start >> 5
        r1 = r0 + 1
        r2 = jnp.minimum(r0 + 2, rows // 32 - 1)
        late = lax.broadcasted_iota(jnp.int32, (32, SLAB), 0) < (start & 31)

        def window(ref):
            blocks = []
            for place in slabs:
                if place is None:
                    blocks.append(jnp.zeros((64, SLAB), BF16))
                    continue
                cols = pl.ds(place * SLAB, SLAB)
                b0, b1, b2 = ref[r0, :, cols], ref[r1, :, cols], ref[r2, :, cols]
                blocks.append(jnp.concatenate([jnp.where(late, b1, b0), jnp.where(late, b2, b1)], axis=0))
            return jnp.concatenate(blocks, axis=1)

        w = window(wz)
        v = window(wv)
        width = SLAB * len(slabs)
        n = width - 128
        right = jnp.concatenate([w[:, :n], v[:, :n], w[:, 128:], v[:, 128:]], axis=0)
        prod = jnp.dot(lhs[shard * TD + k], right, preferred_element_type=F32)
        prod = prod[:32] + left(prod[32:], 32)
        prod = prod[:16] + left(prod[16:], 16)
        prod = prod[:8] + left(prod[8:], 8)
        prod = pltpu.roll(prod, n - 7, 1, stride=1, stride_axis=0)
        wide_w = w.astype(F32)
        return prod[:, : n - 128], jnp.sum((wide_w * wide_w).reshape(8, 8, width), axis=0)

    def window_energy(squares, width):
        high = squares.astype(BF16)
        rest = squares - high.astype(F32)
        mid = rest.astype(BF16)
        low = (rest - mid.astype(F32)).astype(BF16)
        sums = jnp.dot(
            jnp.concatenate([high, mid, low], axis=0), band[:width, : width - SLAB], preferred_element_type=F32
        )
        return sums[:TD] + sums[TD : 2 * TD] + sums[2 * TD :]

    arrivals(0)
    for side in range(2):
        shard = (GROUP + 1) * side
        for k in range(TD):
            cross, squares = correlate(shard, k, ((0, 1), (2, None))[side])
            cb[k, :, :SLAB] = cross
            qb[k, :, : 2 * SLAB] = squares
        cross = jnp.sum(cb[:, :, :SLAB], axis=1)
        energy = window_energy(jnp.sum(qb[:, :, : 2 * SLAB], axis=1), 2 * SLAB)
        if side == 0:
            cross = jnp.where(m == 0, 0.0, cross)
            energy = jnp.where(m == 0, 0.0, energy)
        for half in range(2):
            hs[side, 0, half] = cross[:, half * 128 : (half + 1) * 128]
            hs[side, 1, half] = energy[:, half * 128 : (half + 1) * 128]
        halo(side, "r").start()

    def result_copy(sub, source):
        return pltpu.make_async_remote_copy(
            src_ref=rs.at[sub], dst_ref=rr.at[source], send_sem=r_s.at[sub], recv_sem=r_r.at[source],
            device_id=peer(sub), device_id_type=MESH,
        )

    arrivals(1)
    for side in range(2):
        halo(side, "r").wait()

    def own_shard(own, carry):
        first = jnp.where(own == 0, 0, jnp.where(own == 1, 1, own + 1))
        middle = jnp.where(own == 0, 1, jnp.where(own == 3, 2, own + 2))
        last = jnp.where(own == 0, 3, jnp.where(own == 1, 4, jnp.where(own == 2, 2, 5)))
        for k in range(TD):
            cross, squares = correlate(1 + own, k, (first, middle, last))
            cb[k] = cross
            qb[k] = squares
        cross = jnp.sum(cb[...], axis=1)
        energy = window_energy(jnp.sum(qb[...], axis=1), 3 * SLAB)
        for tile in range(4):
            visit, half = 1 - tile // 2, tile % 2
            for kind, value in enumerate((cross, energy)):
                value = value[:, tile * 128 : (tile + 1) * 128]
                if visit == 1:
                    value = jnp.where((own == 0) & (m == 0), 0.0, value)
                    value = value + jnp.where(own == 0, hr[1, kind, half], 0.0)
                else:
                    value = value + jnp.where(own == GROUP - 1, hr[0, kind, half], 0.0)
                rs[2 * own + half, kind, visit] = value
        for half in range(2):
            sub = 2 * own + half

            @pl.when(sub != d)
            def _():
                result_copy(sub, d).start()

        return carry

    lax.fori_loop(0, GROUP, own_shard, 0)
    rr[d] = rs[d]

    def end_result(i, carry):
        sub = lax.rem(d + i, SUBS)
        result_copy(sub, sub).wait()
        return carry

    lax.fori_loop(1, SUBS, end_result, 0)
    summed = rr[0]
    for sub in range(1, SUBS):
        summed = summed + rr[sub]
    score = summed[0] / jnp.sqrt(summed[1] / (CSPAN * TLEN) + EPS_ENERGY)
    for visit in range(2):
        o_ref[:, visit, :] = score[visit]


def shards(record, templates, offsets):
    ng = lax.axis_size("blk") // GROUP
    samples = record.shape[1]
    rows = CHUNK * ng
    buffer = (GROUP + 2) * SLAB
    tables = jnp.asarray(transform_tables())
    hbm = pl.BlockSpec(memory_space=pl.ANY)
    dma = pltpu.SemaphoreType.DMA
    return pl.pallas_call(
        functools.partial(kernel, ng),
        out_shape=jax.ShapeDtypeStruct((TD, 2, SLAB // 2), F32),
        in_specs=[hbm, hbm, hbm, hbm],
        out_specs=pl.BlockSpec(memory_space=pltpu.VMEM),
        scratch_shapes=[
            pltpu.VMEM(record.shape, F32),
            pltpu.VMEM(templates.shape, BF16),
            pltpu.SMEM(offsets.shape, jnp.int32),
            pltpu.VMEM(tables.shape, F32),
            pltpu.VMEM((samples // FRAME * CHUNK, FRAME), F32),
            pltpu.VMEM((CHUNK, samples), BF16),
            pltpu.VMEM((2, ng, CHUNK, 2 * SLAB), BF16),
            pltpu.VMEM((rows // 32, 32, buffer), BF16),
            pltpu.VMEM((rows // 32, 32, buffer), BF16),
            pltpu.VMEM((SUBS, TD, 32, TLEN), BF16),
            pltpu.VMEM((SUBS, TD, 32, TLEN), BF16),
            pltpu.VMEM((2, 2, TD, 32, TLEN), BF16),
            pltpu.VMEM(((GROUP + 2) * TD, FOLD, 256), BF16),
            pltpu.VMEM((3 * SLAB, 2 * SLAB), BF16),
            pltpu.VMEM((GROUP + 2, TD, 128), jnp.int32),
            pltpu.SMEM((GROUP + 2, TD, 128), jnp.int32),
            pltpu.VMEM((TD, 8, 2 * SLAB), F32),
            pltpu.VMEM((TD, 8, 3 * SLAB), F32),
            pltpu.VMEM((2, 2, 2, TD, 128), F32),
            pltpu.VMEM((2, 2, 2, TD, 128), F32),
            pltpu.VMEM((SUBS, 2, 2, TD, 128), F32),
            pltpu.VMEM((SUBS, 2, 2, TD, 128), F32),
            dma((2, ng)), dma((2, ng)), dma((SUBS,)), dma((SUBS,)), dma((GROUP,)), dma((GROUP,)),
            dma((2,)), dma((2,)), dma((2,)), dma((2,)), dma((2,)), dma((2,)), dma((SUBS,)), dma((SUBS,)),
            dma((1,)), dma((7,)),
        ],
        compiler_params=pltpu.CompilerParams(
            collective_id=0, has_side_effects=True, vmem_limit_bytes=60 * 2**20
        ),
    )(record, templates, offsets, tables)


def solution(mesh):
    return jax.shard_map(
        shards,
        mesh=mesh,
        in_specs=(P(("blk", "ch"), None), P("blk", "ch", None), P("blk")),
        out_specs=P("blk", None, "ch"),
        check_vma=False,
    )
```

```python
import functools

import jax
import jax.numpy as jnp
import numpy as np
from jax import lax
from jax.experimental import pallas as pl
from jax.experimental.pallas import tpu as pltpu
from jax.sharding import PartitionSpec as P

MESH = pl.DeviceIdType.MESH
F32 = jnp.float32
BF16 = jnp.bfloat16

FRAME = 128
CHUNK = 16
CSPAN = 512
TLEN = 256
SLAB = 256
TD = 8
GROUP = 4
SUBS = 8
FOLD = 64
EPS_POWER = 1e-6
EPS_ENERGY = 1e-5


def transform_tables():
    n = np.arange(FRAME)
    col = np.arange(FRAME)
    freq = np.where(col <= 64, col, col - 64)
    angle = 2.0 * np.pi * ((n[:, None] * freq[None, :]) % FRAME) / FRAME
    basis = np.where(col <= 64, np.cos(angle), np.sin(angle))
    weight = np.where((col == 0) | (col == 64), 1.0, 2.0) / np.sqrt(FRAME)

    return np.stack([basis, (basis * weight).T]).astype(np.float32)


def split_table(table):
    high = table.astype(BF16)
    low = (table - high.astype(F32)).astype(BF16)
    top = jnp.concatenate([high, low], axis=1)
    bottom = jnp.concatenate([high, jnp.zeros_like(high)], axis=1)
    return jnp.concatenate([top, bottom], axis=0)


def split_rows(value):
    high = value.astype(BF16)
    low = (value - high.astype(F32)).astype(BF16)
    return jnp.concatenate([high, low], axis=1)


def left(value, count):
    return pltpu.roll(value, value.shape[1] - count, 1)


def kernel(
    ng, x_hbm, t_hbm, off_hbm, tab_hbm, o_ref,
    x_ref, t_ref, off_ref, tab_ref,
    ys, ws, land, wz, wv, tsend, trecv, thalo, lhs, band, offv, offs, cb, qb, hs, hr, rs, rr,
    a_s, a_r, t_s, t_r, f_s, f_r, th_s, th_r, fh_s, fh_r, h_s, h_r, r_s, r_r, loc, ld,
):
    b = lax.axis_index("blk")
    h = lax.axis_index("ch")
    m = lax.div(b, GROUP)
    e = lax.rem(b, GROUP)
    d = 2 * e + h
    up = lax.rem(m + 1, ng)
    down = lax.rem(m + ng - 1, ng)
    rows = CHUNK * ng
    frames = x_ref.shape[1] // FRAME
    wide = GROUP * SLAB

    def peer(sub):
        return {"blk": GROUP * m + lax.div(sub, 2), "ch": lax.rem(sub, 2)}

    def half_block(group):
        return pl.multiple_of(lax.rem(group, 2) * CHUNK, CHUNK)

    def far(group):
        return {"blk": GROUP * group + e}

    parts = 4
    span = x_ref.shape[1] // parts

    def load(i):
        if i < parts:
            cols = pl.ds(i * span, span)
            return pltpu.make_async_copy(x_hbm.at[:, cols], x_ref.at[:, cols], ld.at[i])
        src, dst = ((off_hbm, off_ref), (t_hbm, t_ref), (tab_hbm, tab_ref))[i - parts]
        return pltpu.make_async_copy(src, dst, ld.at[i])

    for i in (parts, parts + 1, parts + 2, *range(parts)):
        load(i).start()

    bar = pltpu.get_barrier_semaphore()

    def greet_peer(i, carry):
        pl.semaphore_signal(bar, inc=1, device_id=peer(lax.rem(d + i, SUBS)), device_id_type=MESH)
        return carry

    def greet_far(i, carry):
        pl.semaphore_signal(bar, inc=1, device_id=far(lax.rem(m + i, ng)), device_id_type=MESH)
        return carry

    lax.fori_loop(1, SUBS, greet_peer, 0)
    lax.fori_loop(1, ng, greet_far, 0)

    r_id = lax.broadcasted_iota(jnp.int32, (256, 256), 0)
    c_id = lax.broadcasted_iota(jnp.int32, (256, 256), 1)
    slot = 128 * ((r_id >> 4) & 1) + 16 * (r_id >> 5) + (r_id & 15)
    load(parts).wait()
    load(parts + 1).wait()
    for k in range(TD):
        perm = jnp.where(((slot - c_id - off_ref[k]) & 255) == 0, 1.0, 0.0).astype(BF16)
        placed = jnp.dot(perm, t_ref[k], preferred_element_type=F32).astype(BF16)
        for s in range(SUBS):
            tsend[s, k] = placed[32 * s : 32 * s + 32]

    row8 = lax.broadcasted_iota(jnp.int32, (TD, 128), 0)
    own_off = jnp.zeros((TD, 128), jnp.int32)
    for k in range(TD):
        own_off = jnp.where(row8 == k, off_ref[k], own_off)
    offv[1 + e] = own_off

    def template_copy(i):
        sub = lax.rem(d + i, SUBS)
        return pltpu.make_async_remote_copy(
            src_ref=tsend.at[sub], dst_ref=trecv.at[d], send_sem=t_s.at[sub], recv_sem=t_r.at[d],
            device_id=peer(sub), device_id_type=MESH,
        )

    def template_arrival(i):
        sub = lax.rem(d + i, SUBS)
        return pltpu.make_async_remote_copy(
            src_ref=tsend.at[sub], dst_ref=trecv.at[sub], send_sem=t_s.at[sub], recv_sem=t_r.at[sub],
            device_id=peer(sub), device_id_type=MESH,
        )

    def offset_copy(i):
        other = lax.rem(e + i, GROUP)
        return pltpu.make_async_remote_copy(
            src_ref=offv.at[1 + e], dst_ref=offv.at[1 + e], send_sem=f_s.at[other], recv_sem=f_r.at[e],
            device_id={"blk": GROUP * m + other}, device_id_type=MESH,
        )

    def offset_arrival(i):
        other = lax.rem(e + i, GROUP)
        return pltpu.make_async_remote_copy(
            src_ref=offv.at[1 + e], dst_ref=offv.at[1 + other], send_sem=f_s.at[other], recv_sem=f_r.at[other],
            device_id={"blk": GROUP * m + other}, device_id_type=MESH,
        )

    def relayed(shard):
        return (shard == 0) | (shard == GROUP - 1)

    def start_templates(early):
        @pl.when(relayed(e) == early)
        def _():
            def start(i, carry):
                template_copy(i).start()
                return carry

            lax.fori_loop(1, SUBS, start, 0)

    def end_templates(early):
        def end(i, carry):
            @pl.when(relayed(lax.div(lax.rem(d + i, SUBS), 2)) == early)
            def _():
                template_arrival(i).wait_recv()

            @pl.when(relayed(e) == early)
            def _():
                template_arrival(i).wait_send()

            return carry

        lax.fori_loop(1, SUBS, end, 0)

    step = 16
    load(parts + 2).wait()
    wf = split_table(tab_ref[0])

    def forward(i, total):
        part = x_ref[:, pl.ds(pl.multiple_of(i * (step * FRAME), FRAME), step * FRAME)]
        stacked = jnp.concatenate([part[:, f * FRAME : (f + 1) * FRAME] for f in range(step)], axis=0)
        both = jnp.dot(split_rows(stacked), wf, preferred_element_type=F32)
        spec = both[:, :FRAME] + both[:, FRAME:]
        ys[pl.ds(pl.multiple_of(i * (step * CHUNK), 8), step * CHUNK), :] = spec
        return total + jnp.sum((spec * spec).reshape(step, CHUNK, FRAME), axis=0)

    total = jnp.zeros((CHUNK, FRAME), F32)
    turns = frames // step // parts
    for i in range(parts):
        load(i).wait()
        total = lax.fori_loop(i * turns, (i + 1) * turns, forward, total, unroll=4)
    mean = total * (1.0 / frames)
    lane = lax.broadcasted_iota(jnp.int32, (CHUNK, FRAME), 1)
    power = jnp.where((lane & 63) == 0, mean, mean + pltpu.roll(mean, 64, 1))
    amp = 1.0 / jnp.sqrt(power + EPS_POWER)
    wi = split_table(tab_ref[1])

    pl.semaphore_wait(bar, SUBS - 1 + ng - 1)
    for i in range(1, GROUP):
        offset_copy(i).start()
    start_templates(True)

    def sample_copy(t, wave, source):
        cols = 2 * SLAB * wave
        return pltpu.make_async_remote_copy(
            src_ref=ws.at[:, pl.ds(pl.multiple_of(t * wide + cols, FRAME), 2 * SLAB)],
            dst_ref=land.at[wave, source],
            send_sem=a_s.at[wave, t], recv_sem=a_r.at[wave, source], device_id=far(t), device_id_type=MESH,
        )

    def back(wave):
        def turn(i, carry):
            quad = lax.rem(lax.div(m, 4) + i, ng // 4)
            spec = []
            for q in range(4):
                base = (4 * quad + q) * (8 * CHUNK)
                for first, count in (((0, 2), (6, 2)), ((2, 4),))[wave]:
                    spec.append(ys[pl.ds(pl.multiple_of(base + first * CHUNK, 8), count * CHUNK), :])
            spec = jnp.concatenate(spec, axis=0)
            scaled = (spec.reshape(step, CHUNK, FRAME) * amp[None]).reshape(step * CHUNK, FRAME)
            both = jnp.dot(split_rows(scaled), wi, preferred_element_type=F32)
            white = (both[:, :FRAME] + both[:, FRAME:]).astype(BF16)
            for f in range(step):
                at = (4 * quad + f // 4) * wide + 2 * SLAB * wave + (f % 4) * FRAME
                ws[:, pl.ds(pl.multiple_of(at, FRAME), FRAME)] = white[f * CHUNK : (f + 1) * CHUNK]
            for q in range(4):
                t = 4 * quad + q

                @pl.when(t != m)
                def _():
                    sample_copy(t, wave, m).start()

            return carry

        lax.fori_loop(0, ng // 4, turn, 0, unroll=4)
        land[wave, m] = ws[
            :, pl.ds(pl.multiple_of(m * wide + 2 * SLAB * wave, FRAME), 2 * SLAB)
        ]

    back(0)

    wz[:, :, 0:SLAB] = jnp.zeros((rows // 32, 32, SLAB), BF16)
    wz[:, :, 5 * SLAB : 6 * SLAB] = jnp.zeros((rows // 32, 32, SLAB), BF16)
    wv[:, :, 5 * SLAB : 6 * SLAB] = jnp.zeros((rows // 32, 32, SLAB), BF16)
    trecv[d] = tsend[d]

    for i in range(1, GROUP):
        offset_arrival(i).wait()

    end_templates(True)

    def halo(side, kind):
        group = up if side == 0 else down
        first = SUBS - 2 if side == 0 else 0
        shard = GROUP if side == 0 else 1
        if kind == "t":
            src, dst, sems = trecv.at[pl.ds(first, 2)], thalo.at[side], (th_s, th_r)
        elif kind == "f":
            src, dst, sems = offv.at[shard], offv.at[(GROUP + 1) * side], (fh_s, fh_r)
        else:
            src, dst, sems = hs.at[side], hr.at[side], (h_s, h_r)
            group = down if side == 0 else up
        return pltpu.make_async_remote_copy(
            src_ref=src, dst_ref=dst, send_sem=sems[0].at[side], recv_sem=sems[1].at[side],
            device_id=far(group), device_id_type=MESH,
        )

    for side in range(2):
        halo(side, "f").start()
        halo(side, "t").start()

    start_templates(False)
    back(1)

    w_id = lax.broadcasted_iota(jnp.int32, band.shape, 0)
    l_id = lax.broadcasted_iota(jnp.int32, band.shape, 1)
    gap = w_id - l_id
    band[...] = jnp.where((gap >= 0) & (gap < TLEN), 1.0, 0.0).astype(BF16)

    r_id = lax.broadcasted_iota(jnp.int32, (FOLD, TLEN), 0)
    s_id = lax.broadcasted_iota(jnp.int32, (FOLD, TLEN), 1)
    pick = jnp.where((s_id & (FOLD - 1)) == ((r_id & ~7) + 7 - (r_id & 7)), 1.0, 0.0).astype(BF16)
    part = lax.broadcasted_iota(jnp.int32, (2 * FOLD * 2, TLEN), 1) >> 6
    which = lax.broadcasted_iota(jnp.int32, (2 * FOLD * 2, TLEN), 0) >> 6
    keep = jnp.where(part == which, 1.0, 0.0).astype(BF16)

    def left_operand(first, second):
        both = jnp.concatenate([first, second], axis=0)
        spread = jnp.concatenate([both] * 4, axis=0) * keep
        turned = lax.dot_general(pick, spread, (((1,), (1,)), ((), ())), preferred_element_type=F32)
        return turned.astype(BF16)

    end_templates(False)

    def prepare(q, carry):
        shard = lax.div(q, TD)
        k = lax.rem(q, TD)
        lhs[TD + q] = left_operand(trecv[2 * shard, k], trecv[2 * shard + 1, k])
        return carry

    lax.fori_loop(0, GROUP * TD, prepare, 0, unroll=8)

    for side in range(2):
        halo(side, "f").wait()
        halo(side, "t").wait()

    def prepare_halo(q, carry):
        side = lax.div(q, TD)
        k = lax.rem(q, TD)
        lhs[side * (GROUP + 1) * TD + k] = left_operand(thalo[side, 0, k], thalo[side, 1, k])
        return carry

    lax.fori_loop(0, 2 * TD, prepare_halo, 0, unroll=8)
    to_scalar = pltpu.make_async_copy(offv, offs, loc.at[0])
    to_scalar.start()
    to_scalar.wait()

    def shift_slabs(t, wave):
        at = pl.ds(half_block(t), CHUNK)
        row = lax.div(t, 2)

        block = land[wave, t]
        new = 1 + 2 * wave
        wz[row, at, new * SLAB : (new + 2) * SLAB] = block
        one, two = block[:, :SLAB], block[:, SLAB:]

        def put(i, block, after):
            wv[row, at, i * SLAB : (i + 1) * SLAB] = jnp.concatenate([block[:, FOLD:], after[:, :FOLD]], axis=1)

        none = jnp.zeros((CHUNK, SLAB), BF16)
        if wave == 0:
            put(0, none, one)
            put(1, one, none)
            put(2, two, none)
        else:
            put(1, wz[row, at, SLAB : 2 * SLAB], one)
            put(3, one, two)
            put(4, two, wz[row, at, 2 * SLAB : 3 * SLAB])

    def arrivals(wave):
        def arrive(i, carry):
            t = lax.rem(m + i, ng)
            sample_copy(t, wave, t).wait()
            shift_slabs(t, wave)
            return carry

        shift_slabs(m, wave)
        lax.fori_loop(1, ng, arrive, 0)

    def correlate(shard, k, slabs):
        off = offs[shard, k, 0]
        start = 16 * (off >> 7) + jnp.clip((off & 127) - 16 * d, 0, 16)
        r0 = start >> 5
        r1 = r0 + 1
        r2 = jnp.minimum(r0 + 2, rows // 32 - 1)
        late = lax.broadcasted_iota(jnp.int32, (32, SLAB), 0) < (start & 31)

        def window(ref):
            blocks = []
            for place in slabs:
                if place is None:
                    blocks.append(jnp.zeros((64, SLAB), BF16))
                    continue
                cols = pl.ds(place * SLAB, SLAB)
                b0, b1, b2 = ref[r0, :, cols], ref[r1, :, cols], ref[r2, :, cols]
                blocks.append(jnp.concatenate([jnp.where(late, b1, b0), jnp.where(late, b2, b1)], axis=0))
            return jnp.concatenate(blocks, axis=1)

        w = window(wz)
        v = window(wv)
        width = SLAB * len(slabs)
        n = width - 128
        right = jnp.concatenate([w[:, :n], v[:, :n], w[:, 128:], v[:, 128:]], axis=0)
        prod = jnp.dot(lhs[shard * TD + k], right, preferred_element_type=F32)
        prod = prod[:32] + left(prod[32:], 32)
        prod = prod[:16] + left(prod[16:], 16)
        prod = prod[:8] + left(prod[8:], 8)
        prod = pltpu.roll(prod, n - 7, 1, stride=1, stride_axis=0)
        wide_w = w.astype(F32)
        return prod[:, : n - 128], jnp.sum((wide_w * wide_w).reshape(8, 8, width), axis=0)

    def window_energy(squares, width):
        high = squares.astype(BF16)
        rest = squares - high.astype(F32)
        mid = rest.astype(BF16)
        low = (rest - mid.astype(F32)).astype(BF16)
        sums = jnp.dot(
            jnp.concatenate([high, mid, low], axis=0), band[:width, : width - SLAB], preferred_element_type=F32
        )
        return sums[:TD] + sums[TD : 2 * TD] + sums[2 * TD :]

    arrivals(0)
    for side in range(2):
        shard = (GROUP + 1) * side
        for k in range(TD):
            cross, squares = correlate(shard, k, ((0, 1), (2, None))[side])
            cb[k, :, :SLAB] = cross
            qb[k, :, : 2 * SLAB] = squares
        cross = jnp.sum(cb[:, :, :SLAB], axis=1)
        energy = window_energy(jnp.sum(qb[:, :, : 2 * SLAB], axis=1), 2 * SLAB)
        if side == 0:
            cross = jnp.where(m == 0, 0.0, cross)
            energy = jnp.where(m == 0, 0.0, energy)
        for half in range(2):
            hs[side, 0, half] = cross[:, half * 128 : (half + 1) * 128]
            hs[side, 1, half] = energy[:, half * 128 : (half + 1) * 128]
        halo(side, "r").start()

    def result_copy(sub, source):
        return pltpu.make_async_remote_copy(
            src_ref=rs.at[sub], dst_ref=rr.at[source], send_sem=r_s.at[sub], recv_sem=r_r.at[source],
            device_id=peer(sub), device_id_type=MESH,
        )

    arrivals(1)
    for side in range(2):
        halo(side, "r").wait()

    def own_shard(own, carry):
        first = jnp.where(own == 0, 0, jnp.where(own == 1, 1, own + 1))
        middle = jnp.where(own == 0, 1, jnp.where(own == 3, 2, own + 2))
        last = jnp.where(own == 0, 3, jnp.where(own == 1, 4, jnp.where(own == 2, 2, 5)))
        for k in range(TD):
            cross, squares = correlate(1 + own, k, (first, middle, last))
            cb[k] = cross
            qb[k] = squares
        cross = jnp.sum(cb[...], axis=1)
        energy = window_energy(jnp.sum(qb[...], axis=1), 3 * SLAB)
        for tile in range(4):
            visit, half = 1 - tile // 2, tile % 2
            for kind, value in enumerate((cross, energy)):
                value = value[:, tile * 128 : (tile + 1) * 128]
                if visit == 1:
                    value = jnp.where((own == 0) & (m == 0), 0.0, value)
                    value = value + jnp.where(own == 0, hr[1, kind, half], 0.0)
                else:
                    value = value + jnp.where(own == GROUP - 1, hr[0, kind, half], 0.0)
                rs[2 * own + half, kind, visit] = value
        for half in range(2):
            sub = 2 * own + half

            @pl.when(sub != d)
            def _():
                result_copy(sub, d).start()

        return carry

    lax.fori_loop(0, GROUP, own_shard, 0)
    rr[d] = rs[d]

    def end_result(i, carry):
        sub = lax.rem(d + i, SUBS)
        result_copy(sub, sub).wait()
        return carry

    lax.fori_loop(1, SUBS, end_result, 0)
    summed = rr[0]
    for sub in range(1, SUBS):
        summed = summed + rr[sub]
    score = summed[0] / jnp.sqrt(summed[1] / (CSPAN * TLEN) + EPS_ENERGY)
    for visit in range(2):
        o_ref[:, visit, :] = score[visit]


def shards(record, templates, offsets):
    ng = lax.axis_size("blk") // GROUP
    samples = record.shape[1]
    rows = CHUNK * ng
    buffer = (GROUP + 2) * SLAB
    tables = jnp.asarray(transform_tables())
    hbm = pl.BlockSpec(memory_space=pl.ANY)
    dma = pltpu.SemaphoreType.DMA
    return pl.pallas_call(
        functools.partial(kernel, ng),
        out_shape=jax.ShapeDtypeStruct((TD, 2, SLAB // 2), F32),
        in_specs=[hbm, hbm, hbm, hbm],
        out_specs=pl.BlockSpec(memory_space=pltpu.VMEM),
        scratch_shapes=[
            pltpu.VMEM(record.shape, F32),
            pltpu.VMEM(templates.shape, BF16),
            pltpu.SMEM(offsets.shape, jnp.int32),
            pltpu.VMEM(tables.shape, F32),
            pltpu.VMEM((samples // FRAME * CHUNK, FRAME), F32),
            pltpu.VMEM((CHUNK, samples), BF16),
            pltpu.VMEM((2, ng, CHUNK, 2 * SLAB), BF16),
            pltpu.VMEM((rows // 32, 32, buffer), BF16),
            pltpu.VMEM((rows // 32, 32, buffer), BF16),
            pltpu.VMEM((SUBS, TD, 32, TLEN), BF16),
            pltpu.VMEM((SUBS, TD, 32, TLEN), BF16),
            pltpu.VMEM((2, 2, TD, 32, TLEN), BF16),
            pltpu.VMEM(((GROUP + 2) * TD, FOLD, 256), BF16),
            pltpu.VMEM((3 * SLAB, 2 * SLAB), BF16),
            pltpu.VMEM((GROUP + 2, TD, 128), jnp.int32),
            pltpu.SMEM((GROUP + 2, TD, 128), jnp.int32),
            pltpu.VMEM((TD, 8, 2 * SLAB), F32),
            pltpu.VMEM((TD, 8, 3 * SLAB), F32),
            pltpu.VMEM((2, 2, 2, TD, 128), F32),
            pltpu.VMEM((2, 2, 2, TD, 128), F32),
            pltpu.VMEM((SUBS, 2, 2, TD, 128), F32),
            pltpu.VMEM((SUBS, 2, 2, TD, 128), F32),
            dma((2, ng)), dma((2, ng)), dma((SUBS,)), dma((SUBS,)), dma((GROUP,)), dma((GROUP,)),
            dma((2,)), dma((2,)), dma((2,)), dma((2,)), dma((2,)), dma((2,)), dma((SUBS,)), dma((SUBS,)),
            dma((1,)), dma((7,)),
        ],
        compiler_params=pltpu.CompilerParams(
            collective_id=0, has_side_effects=True, vmem_limit_bytes=60 * 2**20
        ),
    )(record, templates, offsets, tables)


def solution(mesh):
    return jax.shard_map(
        shards,
        mesh=mesh,
        in_specs=(P(("blk", "ch"), None), P("blk", "ch", None), P("blk")),
        out_specs=P("blk", None, "ch"),
        check_vma=False,
    )
```

```python
import functools

import jax
import jax.numpy as jnp
import numpy as np
from jax import lax
from jax.experimental import pallas as pl
from jax.experimental.pallas import tpu as pltpu
from jax.sharding import PartitionSpec as P

MESH = pl.DeviceIdType.MESH
F32 = jnp.float32
BF16 = jnp.bfloat16

FRAME = 128
CHUNK = 16
CSPAN = 512
TLEN = 256
SLAB = 256
TD = 8
GROUP = 4
SUBS = 8
FOLD = 64
EPS_POWER = 1e-6
EPS_ENERGY = 1e-5


def transform_tables():
    n = np.arange(FRAME)
    col = np.arange(FRAME)
    freq = np.where(col <= 64, col, col - 64)
    angle = 2.0 * np.pi * ((n[:, None] * freq[None, :]) % FRAME) / FRAME
    basis = np.where(col <= 64, np.cos(angle), np.sin(angle))
    weight = np.where((col == 0) | (col == 64), 1.0, 2.0) / np.sqrt(FRAME)

    return np.stack([basis, (basis * weight).T]).astype(np.float32)


def split_table(table):
    high = table.astype(BF16)
    low = (table - high.astype(F32)).astype(BF16)
    top = jnp.concatenate([high, low], axis=1)
    bottom = jnp.concatenate([high, jnp.zeros_like(high)], axis=1)
    return jnp.concatenate([top, bottom], axis=0)


def split_rows(value):
    high = value.astype(BF16)
    low = (value - high.astype(F32)).astype(BF16)
    return jnp.concatenate([high, low], axis=1)


def left(value, count):
    return pltpu.roll(value, value.shape[1] - count, 1)


def kernel(
    ng, x_hbm, t_hbm, off_hbm, tab_hbm, o_ref,
    x_ref, t_ref, off_ref, tab_ref,
    ys, ws, land, wz, wv, tsend, trecv, thalo, lhs, band, offv, offs, cb, qb, hs, hr, rs, rr,
    a_s, a_r, t_s, t_r, f_s, f_r, th_s, th_r, fh_s, fh_r, h_s, h_r, r_s, r_r, loc, ld,
):
    b = lax.axis_index("blk")
    h = lax.axis_index("ch")
    m = lax.div(b, GROUP)
    e = lax.rem(b, GROUP)
    d = 2 * e + h
    up = lax.rem(m + 1, ng)
    down = lax.rem(m + ng - 1, ng)
    rows = CHUNK * ng
    frames = x_ref.shape[1] // FRAME
    wide = GROUP * SLAB

    def peer(sub):
        return {"blk": GROUP * m + lax.div(sub, 2), "ch": lax.rem(sub, 2)}

    def half_block(group):
        return pl.multiple_of(lax.rem(group, 2) * CHUNK, CHUNK)

    def far(group):
        return {"blk": GROUP * group + e}

    parts = 4
    span = x_ref.shape[1] // parts

    def load(i):
        if i < parts:
            cols = pl.ds(i * span, span)
            return pltpu.make_async_copy(x_hbm.at[:, cols], x_ref.at[:, cols], ld.at[i])
        src, dst = ((off_hbm, off_ref), (t_hbm, t_ref), (tab_hbm, tab_ref))[i - parts]
        return pltpu.make_async_copy(src, dst, ld.at[i])

    for i in (parts, parts + 1, parts + 2, *range(parts)):
        load(i).start()

    bar = pltpu.get_barrier_semaphore()

    def greet_peer(i, carry):
        pl.semaphore_signal(bar, inc=1, device_id=peer(lax.rem(d + i, SUBS)), device_id_type=MESH)
        return carry

    def greet_far(i, carry):
        pl.semaphore_signal(bar, inc=1, device_id=far(lax.rem(m + i, ng)), device_id_type=MESH)
        return carry

    lax.fori_loop(1, SUBS, greet_peer, 0)
    lax.fori_loop(1, ng, greet_far, 0)

    r_id = lax.broadcasted_iota(jnp.int32, (256, 256), 0)
    c_id = lax.broadcasted_iota(jnp.int32, (256, 256), 1)
    slot = 128 * ((r_id >> 4) & 1) + 16 * (r_id >> 5) + (r_id & 15)
    load(parts).wait()
    load(parts + 1).wait()
    for k in range(TD):
        perm = jnp.where(((slot - c_id - off_ref[k]) & 255) == 0, 1.0, 0.0).astype(BF16)
        placed = jnp.dot(perm, t_ref[k], preferred_element_type=F32).astype(BF16)
        for s in range(SUBS):
            tsend[s, k] = placed[32 * s : 32 * s + 32]

    row8 = lax.broadcasted_iota(jnp.int32, (TD, 128), 0)
    own_off = jnp.zeros((TD, 128), jnp.int32)
    for k in range(TD):
        own_off = jnp.where(row8 == k, off_ref[k], own_off)
    offv[1 + e] = own_off

    def template_copy(i):
        sub = lax.rem(d + i, SUBS)
        return pltpu.make_async_remote_copy(
            src_ref=tsend.at[sub], dst_ref=trecv.at[d], send_sem=t_s.at[sub], recv_sem=t_r.at[d],
            device_id=peer(sub), device_id_type=MESH,
        )

    def template_arrival(i):
        sub = lax.rem(d + i, SUBS)
        return pltpu.make_async_remote_copy(
            src_ref=tsend.at[sub], dst_ref=trecv.at[sub], send_sem=t_s.at[sub], recv_sem=t_r.at[sub],
            device_id=peer(sub), device_id_type=MESH,
        )

    def offset_copy(i):
        other = lax.rem(e + i, GROUP)
        return pltpu.make_async_remote_copy(
            src_ref=offv.at[1 + e], dst_ref=offv.at[1 + e], send_sem=f_s.at[other], recv_sem=f_r.at[e],
            device_id={"blk": GROUP * m + other}, device_id_type=MESH,
        )

    def offset_arrival(i):
        other = lax.rem(e + i, GROUP)
        return pltpu.make_async_remote_copy(
            src_ref=offv.at[1 + e], dst_ref=offv.at[1 + other], send_sem=f_s.at[other], recv_sem=f_r.at[other],
            device_id={"blk": GROUP * m + other}, device_id_type=MESH,
        )

    def relayed(shard):
        return (shard == 0) | (shard == GROUP - 1)

    def start_templates(early):
        @pl.when(relayed(e) == early)
        def _():
            def start(i, carry):
                template_copy(i).start()
                return carry

            lax.fori_loop(1, SUBS, start, 0)

    def end_templates(early):
        def end(i, carry):
            @pl.when(relayed(lax.div(lax.rem(d + i, SUBS), 2)) == early)
            def _():
                template_arrival(i).wait_recv()

            @pl.when(relayed(e) == early)
            def _():
                template_arrival(i).wait_send()

            return carry

        lax.fori_loop(1, SUBS, end, 0)

    step = 16
    load(parts + 2).wait()
    wf = split_table(tab_ref[0])

    def forward(i, total):
        part = x_ref[:, pl.ds(pl.multiple_of(i * (step * FRAME), FRAME), step * FRAME)]
        stacked = jnp.concatenate([part[:, f * FRAME : (f + 1) * FRAME] for f in range(step)], axis=0)
        both = jnp.dot(split_rows(stacked), wf, preferred_element_type=F32)
        spec = both[:, :FRAME] + both[:, FRAME:]
        ys[pl.ds(pl.multiple_of(i * (step * CHUNK), 8), step * CHUNK), :] = spec
        return total + jnp.sum((spec * spec).reshape(step, CHUNK, FRAME), axis=0)

    total = jnp.zeros((CHUNK, FRAME), F32)
    turns = frames // step // parts
    for i in range(parts):
        load(i).wait()
        total = lax.fori_loop(i * turns, (i + 1) * turns, forward, total, unroll=4)
    mean = total * (1.0 / frames)
    lane = lax.broadcasted_iota(jnp.int32, (CHUNK, FRAME), 1)
    power = jnp.where((lane & 63) == 0, mean, mean + pltpu.roll(mean, 64, 1))
    amp = 1.0 / jnp.sqrt(power + EPS_POWER)
    wi = split_table(tab_ref[1])

    pl.semaphore_wait(bar, SUBS - 1 + ng - 1)
    for i in range(1, GROUP):
        offset_copy(i).start()
    start_templates(True)

    def sample_copy(t, wave, source):
        cols = 2 * SLAB * wave
        return pltpu.make_async_remote_copy(
            src_ref=ws.at[:, pl.ds(pl.multiple_of(t * wide + cols, FRAME), 2 * SLAB)],
            dst_ref=land.at[wave, source],
            send_sem=a_s.at[wave, t], recv_sem=a_r.at[wave, source], device_id=far(t), device_id_type=MESH,
        )

    def back(wave):
        def turn(i, carry):
            quad = lax.rem(lax.div(m, 4) + i, ng // 4)
            spec = []
            for q in range(4):
                base = (4 * quad + q) * (8 * CHUNK)
                for first, count in (((0, 2), (6, 2)), ((2, 4),))[wave]:
                    spec.append(ys[pl.ds(pl.multiple_of(base + first * CHUNK, 8), count * CHUNK), :])
            spec = jnp.concatenate(spec, axis=0)
            scaled = (spec.reshape(step, CHUNK, FRAME) * amp[None]).reshape(step * CHUNK, FRAME)
            both = jnp.dot(split_rows(scaled), wi, preferred_element_type=F32)
            white = (both[:, :FRAME] + both[:, FRAME:]).astype(BF16)
            for f in range(step):
                at = (4 * quad + f // 4) * wide + 2 * SLAB * wave + (f % 4) * FRAME
                ws[:, pl.ds(pl.multiple_of(at, FRAME), FRAME)] = white[f * CHUNK : (f + 1) * CHUNK]
            for q in range(4):
                t = 4 * quad + q

                @pl.when(t != m)
                def _():
                    sample_copy(t, wave, m).start()

            return carry

        lax.fori_loop(0, ng // 4, turn, 0, unroll=4)
        land[wave, m] = ws[
            :, pl.ds(pl.multiple_of(m * wide + 2 * SLAB * wave, FRAME), 2 * SLAB)
        ]

    back(0)

    wz[:, :, 0:SLAB] = jnp.zeros((rows // 32, 32, SLAB), BF16)
    wz[:, :, 5 * SLAB : 6 * SLAB] = jnp.zeros((rows // 32, 32, SLAB), BF16)
    wv[:, :, 5 * SLAB : 6 * SLAB] = jnp.zeros((rows // 32, 32, SLAB), BF16)
    trecv[d] = tsend[d]

    for i in range(1, GROUP):
        offset_arrival(i).wait()

    end_templates(True)

    def halo(side, kind):
        group = up if side == 0 else down
        first = SUBS - 2 if side == 0 else 0
        shard = GROUP if side == 0 else 1
        if kind == "t":
            src, dst, sems = trecv.at[pl.ds(first, 2)], thalo.at[side], (th_s, th_r)
        elif kind == "f":
            src, dst, sems = offv.at[shard], offv.at[(GROUP + 1) * side], (fh_s, fh_r)
        else:
            src, dst, sems = hs.at[side], hr.at[side], (h_s, h_r)
            group = down if side == 0 else up
        return pltpu.make_async_remote_copy(
            src_ref=src, dst_ref=dst, send_sem=sems[0].at[side], recv_sem=sems[1].at[side],
            device_id=far(group), device_id_type=MESH,
        )

    for side in range(2):
        halo(side, "f").start()
        halo(side, "t").start()

    start_templates(False)
    back(1)

    w_id = lax.broadcasted_iota(jnp.int32, band.shape, 0)
    l_id = lax.broadcasted_iota(jnp.int32, band.shape, 1)
    gap = w_id - l_id
    band[...] = jnp.where((gap >= 0) & (gap < TLEN), 1.0, 0.0).astype(BF16)

    r_id = lax.broadcasted_iota(jnp.int32, (FOLD, TLEN), 0)
    s_id = lax.broadcasted_iota(jnp.int32, (FOLD, TLEN), 1)
    pick = jnp.where((s_id & (FOLD - 1)) == ((r_id & ~7) + 7 - (r_id & 7)), 1.0, 0.0).astype(BF16)
    part = lax.broadcasted_iota(jnp.int32, (2 * FOLD * 2, TLEN), 1) >> 6
    which = lax.broadcasted_iota(jnp.int32, (2 * FOLD * 2, TLEN), 0) >> 6
    keep = jnp.where(part == which, 1.0, 0.0).astype(BF16)

    def left_operand(first, second):
        both = jnp.concatenate([first, second], axis=0)
        spread = jnp.concatenate([both] * 4, axis=0) * keep
        turned = lax.dot_general(pick, spread, (((1,), (1,)), ((), ())), preferred_element_type=F32)
        return turned.astype(BF16)

    end_templates(False)

    def prepare(q, carry):
        shard = lax.div(q, TD)
        k = lax.rem(q, TD)
        lhs[TD + q] = left_operand(trecv[2 * shard, k], trecv[2 * shard + 1, k])
        return carry

    lax.fori_loop(0, GROUP * TD, prepare, 0, unroll=8)

    for side in range(2):
        halo(side, "f").wait()
        halo(side, "t").wait()

    def prepare_halo(q, carry):
        side = lax.div(q, TD)
        k = lax.rem(q, TD)
        lhs[side * (GROUP + 1) * TD + k] = left_operand(thalo[side, 0, k], thalo[side, 1, k])
        return carry

    lax.fori_loop(0, 2 * TD, prepare_halo, 0, unroll=8)
    to_scalar = pltpu.make_async_copy(offv, offs, loc.at[0])
    to_scalar.start()
    to_scalar.wait()

    def shift_slabs(t, wave):
        at = pl.ds(half_block(t), CHUNK)
        row = lax.div(t, 2)

        block = land[wave, t]
        new = 1 + 2 * wave
        wz[row, at, new * SLAB : (new + 2) * SLAB] = block
        one, two = block[:, :SLAB], block[:, SLAB:]

        def put(i, block, after):
            wv[row, at, i * SLAB : (i + 1) * SLAB] = jnp.concatenate([block[:, FOLD:], after[:, :FOLD]], axis=1)

        none = jnp.zeros((CHUNK, SLAB), BF16)
        if wave == 0:
            put(0, none, one)
            put(1, one, none)
            put(2, two, none)
        else:
            put(1, wz[row, at, SLAB : 2 * SLAB], one)
            put(3, one, two)
            put(4, two, wz[row, at, 2 * SLAB : 3 * SLAB])

    def arrivals(wave):
        def arrive(i, carry):
            t = lax.rem(m + i, ng)
            sample_copy(t, wave, t).wait()
            return carry

        def shift(t, carry):
            shift_slabs(t, wave)
            return carry

        lax.fori_loop(1, ng, arrive, 0)
        lax.fori_loop(0, ng, shift, 0, unroll=8)

    def correlate(shard, k, slabs):
        off = offs[shard, k, 0]
        start = 16 * (off >> 7) + jnp.clip((off & 127) - 16 * d, 0, 16)
        r0 = start >> 5
        r1 = r0 + 1
        r2 = jnp.minimum(r0 + 2, rows // 32 - 1)
        late = lax.broadcasted_iota(jnp.int32, (32, SLAB), 0) < (start & 31)

        def window(ref):
            blocks = []
            for place in slabs:
                if place is None:
                    blocks.append(jnp.zeros((64, SLAB), BF16))
                    continue
                cols = pl.ds(place * SLAB, SLAB)
                b0, b1, b2 = ref[r0, :, cols], ref[r1, :, cols], ref[r2, :, cols]
                blocks.append(jnp.concatenate([jnp.where(late, b1, b0), jnp.where(late, b2, b1)], axis=0))
            return jnp.concatenate(blocks, axis=1)

        w = window(wz)
        v = window(wv)
        width = SLAB * len(slabs)
        n = width - 128
        right = jnp.concatenate([w[:, :n], v[:, :n], w[:, 128:], v[:, 128:]], axis=0)
        prod = jnp.dot(lhs[shard * TD + k], right, preferred_element_type=F32)
        prod = prod[:32] + left(prod[32:], 32)
        prod = prod[:16] + left(prod[16:], 16)
        prod = prod[:8] + left(prod[8:], 8)
        prod = pltpu.roll(prod, n - 7, 1, stride=1, stride_axis=0)
        wide_w = w.astype(F32)
        return prod[:, : n - 128], jnp.sum((wide_w * wide_w).reshape(8, 8, width), axis=0)

    def window_energy(squares, width):
        high = squares.astype(BF16)
        rest = squares - high.astype(F32)
        mid = rest.astype(BF16)
        low = (rest - mid.astype(F32)).astype(BF16)
        sums = jnp.dot(
            jnp.concatenate([high, mid, low], axis=0), band[:width, : width - SLAB], preferred_element_type=F32
        )
        return sums[:TD] + sums[TD : 2 * TD] + sums[2 * TD :]

    arrivals(0)
    for side in range(2):
        shard = (GROUP + 1) * side
        for k in range(TD):
            cross, squares = correlate(shard, k, ((0, 1), (2, None))[side])
            cb[k, :, :SLAB] = cross
            qb[k, :, : 2 * SLAB] = squares
        cross = jnp.sum(cb[:, :, :SLAB], axis=1)
        energy = window_energy(jnp.sum(qb[:, :, : 2 * SLAB], axis=1), 2 * SLAB)
        if side == 0:
            cross = jnp.where(m == 0, 0.0, cross)
            energy = jnp.where(m == 0, 0.0, energy)
        for half in range(2):
            hs[side, 0, half] = cross[:, half * 128 : (half + 1) * 128]
            hs[side, 1, half] = energy[:, half * 128 : (half + 1) * 128]
        halo(side, "r").start()

    def result_copy(sub, source):
        return pltpu.make_async_remote_copy(
            src_ref=rs.at[sub], dst_ref=rr.at[source], send_sem=r_s.at[sub], recv_sem=r_r.at[source],
            device_id=peer(sub), device_id_type=MESH,
        )

    arrivals(1)
    for side in range(2):
        halo(side, "r").wait()

    def own_shard(own, carry):
        first = jnp.where(own == 0, 0, jnp.where(own == 1, 1, own + 1))
        middle = jnp.where(own == 0, 1, jnp.where(own == 3, 2, own + 2))
        last = jnp.where(own == 0, 3, jnp.where(own == 1, 4, jnp.where(own == 2, 2, 5)))
        for k in range(TD):
            cross, squares = correlate(1 + own, k, (first, middle, last))
            cb[k] = cross
            qb[k] = squares
        cross = jnp.sum(cb[...], axis=1)
        energy = window_energy(jnp.sum(qb[...], axis=1), 3 * SLAB)
        for tile in range(4):
            visit, half = 1 - tile // 2, tile % 2
            for kind, value in enumerate((cross, energy)):
                value = value[:, tile * 128 : (tile + 1) * 128]
                if visit == 1:
                    value = jnp.where((own == 0) & (m == 0), 0.0, value)
                    value = value + jnp.where(own == 0, hr[1, kind, half], 0.0)
                else:
                    value = value + jnp.where(own == GROUP - 1, hr[0, kind, half], 0.0)
                rs[2 * own + half, kind, visit] = value
        for half in range(2):
            sub = 2 * own + half

            @pl.when(sub != d)
            def _():
                result_copy(sub, d).start()

        return carry

    lax.fori_loop(0, GROUP, own_shard, 0)
    rr[d] = rs[d]

    def end_result(i, carry):
        sub = lax.rem(d + i, SUBS)
        result_copy(sub, sub).wait()
        return carry

    lax.fori_loop(1, SUBS, end_result, 0)
    summed = rr[0]
    for sub in range(1, SUBS):
        summed = summed + rr[sub]
    score = summed[0] / jnp.sqrt(summed[1] / (CSPAN * TLEN) + EPS_ENERGY)
    for visit in range(2):
        o_ref[:, visit, :] = score[visit]


def shards(record, templates, offsets):
    ng = lax.axis_size("blk") // GROUP
    samples = record.shape[1]
    rows = CHUNK * ng
    buffer = (GROUP + 2) * SLAB
    tables = jnp.asarray(transform_tables())
    hbm = pl.BlockSpec(memory_space=pl.ANY)
    dma = pltpu.SemaphoreType.DMA
    return pl.pallas_call(
        functools.partial(kernel, ng),
        out_shape=jax.ShapeDtypeStruct((TD, 2, SLAB // 2), F32),
        in_specs=[hbm, hbm, hbm, hbm],
        out_specs=pl.BlockSpec(memory_space=pltpu.VMEM),
        scratch_shapes=[
            pltpu.VMEM(record.shape, F32),
            pltpu.VMEM(templates.shape, BF16),
            pltpu.SMEM(offsets.shape, jnp.int32),
            pltpu.VMEM(tables.shape, F32),
            pltpu.VMEM((samples // FRAME * CHUNK, FRAME), F32),
            pltpu.VMEM((CHUNK, samples), BF16),
            pltpu.VMEM((2, ng, CHUNK, 2 * SLAB), BF16),
            pltpu.VMEM((rows // 32, 32, buffer), BF16),
            pltpu.VMEM((rows // 32, 32, buffer), BF16),
            pltpu.VMEM((SUBS, TD, 32, TLEN), BF16),
            pltpu.VMEM((SUBS, TD, 32, TLEN), BF16),
            pltpu.VMEM((2, 2, TD, 32, TLEN), BF16),
            pltpu.VMEM(((GROUP + 2) * TD, FOLD, 256), BF16),
            pltpu.VMEM((3 * SLAB, 2 * SLAB), BF16),
            pltpu.VMEM((GROUP + 2, TD, 128), jnp.int32),
            pltpu.SMEM((GROUP + 2, TD, 128), jnp.int32),
            pltpu.VMEM((TD, 8, 2 * SLAB), F32),
            pltpu.VMEM((TD, 8, 3 * SLAB), F32),
            pltpu.VMEM((2, 2, 2, TD, 128), F32),
            pltpu.VMEM((2, 2, 2, TD, 128), F32),
            pltpu.VMEM((SUBS, 2, 2, TD, 128), F32),
            pltpu.VMEM((SUBS, 2, 2, TD, 128), F32),
            dma((2, ng)), dma((2, ng)), dma((SUBS,)), dma((SUBS,)), dma((GROUP,)), dma((GROUP,)),
            dma((2,)), dma((2,)), dma((2,)), dma((2,)), dma((2,)), dma((2,)), dma((SUBS,)), dma((SUBS,)),
            dma((1,)), dma((7,)),
        ],
        compiler_params=pltpu.CompilerParams(
            collective_id=0, has_side_effects=True, vmem_limit_bytes=60 * 2**20
        ),
    )(record, templates, offsets, tables)


def solution(mesh):
    return jax.shard_map(
        shards,
        mesh=mesh,
        in_specs=(P(("blk", "ch"), None), P("blk", "ch", None), P("blk")),
        out_specs=P("blk", None, "ch"),
        check_vma=False,
    )
```
